512 devices in a mesh: band: 4 (over x), dx: 8 (over y), dyz: 16 (over z, core).
Axes of the slice: x: 4, y: 8, z: 8, core: 2. Of those that a mesh axis runs over, the one named last changes fastest.
Arguments:
- density: float32 [256, 384, 512], P('dx', 'dyz', 'band'), may hold values from 0.1 to 3
- hartree: float32 [256, 384, 512], P('dx', 'dyz', 'band'), may hold values from -6 to 6
- box_root: int32 [3, 8192], P(None, ('dx', 'dyz')), may hold values from 0 to 511, as said below
- species: int32 [8192], P(('dx', 'dyz')), may hold values from 0 to 1
- atom_count: int32 [128], P(('dx', 'dyz')), may hold values from 1 to 64, 4096 in all
- shape_functions: float32 [2, 25, 4096], replicated, may hold values from -28 to 28
- coupling: float32 [2, 25, 256], replicated, may hold values from -1.25 to 1.25
- coulomb: float32 [2, 256, 256], replicated, may hold values from -0.375 to 0.375
- rho_ij: float32 [8192, 256], P(('dx', 'dyz')), may hold values from -6 to 6
- projections: float32 [8192, 16, 512], P(('dx', 'dyz'), None, 'band'), may hold values from -6 to 6
Outputs:
- potential: float32 [256, 384, 512], P('dx', 'dyz', 'band')
- atom_hamiltonian: float32 [8192, 256], P(('dx', 'dyz'))
- applied: float32 [8192, 16, 512], P(('dx', 'dyz'), None, 'band')
The draws below stay inside these ranges and needn't reach their ends.
Inputs may be any that keep to these rules, and one draw needn't show every extreme that they name: Atom a's first two box_root entries lie within the first- and second-dimension cells held by the devices that hold atom a; the third is any cell of the third dimension. Domain column c holds its atoms in slots c * 64 to c * 64 + atom_count[c] - 1; its other slots are empty.
All inputs are finite; a program needn't handle non-finite values. No bound on the sum of `atom_count` on one device may be relied on, other than what follows from the above.
Results may differ from the reference program's by a relative error of at most 0.0003.
Values sent between devices are 32-bit elements; how exact they have to be, the bound alone decides.
No kernel may reach another device: no remote copies, remote signals or barrier semaphores. Data moves between devices by JAX's collectives and lax.ppermute only.
A program may use at most 64 MiB of HBM per device.

```python
import math
import jax
import jax.numpy as jnp
import numpy as np
from jax import lax

CX = 32
CY = 24
BOX = 16
NL = 25
NI = 16
NSPEC = 2
ATOM_DEV = 64
NX = 256
NY = 384
NZ = 512
COLUMNS = 128
ATOMS = 8192
BANDS = 512
N_DYZ = 16


def draw_box_root(key, part):
    key = jax.random.fold_in(key, 11)
    slots = jnp.arange(ATOMS, dtype=jnp.int32)
    column = slots // ATOM_DEV
    start_x = column // N_DYZ * CX
    start_y = column % N_DYZ * CY
    keys = jax.random.split(key, 3)
    offset_x = jax.random.randint(keys[0], (ATOMS,), 0, CX, dtype=jnp.int32)
    offset_y = jax.random.randint(keys[1], (ATOMS,), 0, CY, dtype=jnp.int32)
    offset_z = jax.random.randint(keys[2], (ATOMS,), 0, NZ, dtype=jnp.int32)
    offset_x = offset_x.at[0].set(0).at[ATOMS - 1].set(CX - 1)
    offset_y = offset_y.at[0].set(0).at[ATOMS - 1].set(CY - 1)
    offset_z = offset_z.at[0].set(0).at[ATOMS - 1].set(NZ - 1)
    return jnp.stack([start_x + offset_x, start_y + offset_y, offset_z]).astype(jnp.int32)


def set_ends(values, stream_key, smallest, high):
    index_at = [jax.random.randint(jax.random.fold_in(stream_key, axis), (), 0, length) for axis, length in enumerate(values.shape)]
    main_axis = values.shape.index(max(values.shape))
    beside = index_at[:main_axis] + [(index_at[main_axis] + 1) % values.shape[main_axis]] + index_at[main_axis + 1:]
    return values.at[tuple(index_at)].set(smallest).at[tuple(beside)].set(high)


def level_of(own_key, shape, cuts, smallest, top_value):
    factor_of = 1.0
    for dim, blocks in cuts:
        steps = jax.random.uniform(jax.random.fold_in(jax.random.fold_in(own_key, 6), dim), (blocks,), jnp.float32, smallest / len(cuts), top_value / len(cuts))
        factor_of = factor_of * jnp.repeat(jnp.exp(steps), shape[dim] // blocks).reshape((-1,) + (1,) * (len(shape) - 1 - dim))
    return factor_of


def profile(number_of, total, most, lean):
    loads = [(1 << 20) // math.isqrt(rank ** lean) + 1 for rank in range(2, number_of + 1)]
    spare, given = total - most - (number_of - 1), [1] * (number_of - 1)
    while spare > 0:
        free = [i for i in range(number_of - 1) if given[i] < most]
        pool, remaining = sum([loads[i] for i in free]), spare
        for i in free:
            addition = min(most - given[i], max(1, remaining * loads[i] // pool), spare)
            given[i] = given[i] + addition
            spare = spare - addition
    return np.array([most] + given)


def uneven_parts(rng, number_of, total, most, lean):
    if number_of == 2:
        one = jax.random.randint(rng, (), max(1, total - most), min(most, total - 1) + 1)
        return jnp.stack([one, total - one])
    lengths = jnp.asarray(profile(number_of, total, most, lean), jnp.int32)
    twos = (number_of - 1) // 2
    donor, sink = lengths[1:1 + 2 * twos:2], lengths[2:2 + 2 * twos:2]
    margin = jnp.minimum(donor - 1, most - sink)
    passed = jax.random.randint(jax.random.fold_in(rng, 1), (twos,), 0, 1 << 20) % (margin + 1)
    lengths = lengths.at[1:1 + 2 * twos:2].set(donor - passed).at[2:2 + 2 * twos:2].set(sink + passed)
    return lengths[jax.random.permutation(jax.random.fold_in(rng, 2), number_of)]


def gaussian(stream_key, extent, width, most, pieces=(), held_as=jnp.bfloat16):
    array = width * jax.random.normal(stream_key, extent, jnp.float32)
    if pieces:
        array = array * level_of(stream_key, extent, pieces, -0.22, 0.18)
    return jnp.clip(array, -most, most).astype(held_as)


def setup_inputs(seed: int = 0) -> dict:
    splits = jax.random.split(jax.random.key(seed), 11)
    return {
        "density": jnp.clip(jnp.exp(math.log(3.0) - 3.4011974 * jax.random.uniform(splits[0], (NX, NY, NZ), jnp.float32) ** level_of(splits[0], (NX, NY, NZ), ((0, 8), (1, 16), (2, 4)), -0.2, 0.2)), 0.1, 3.0),
        "hartree": gaussian(splits[1], (NX, NY, NZ), 1.0, 6.0, ((0, 8), (1, 16), (2, 4)), jnp.float32),
        "box_root": draw_box_root(jax.random.fold_in(splits[10], 71), 0),
        "species": set_ends(jax.random.randint(splits[3], (ATOMS,), 0, NSPEC), jax.random.fold_in(splits[3], 1), 0, NSPEC - 1).astype(jnp.int32),
        "atom_count": uneven_parts(splits[4], COLUMNS, COLUMNS * ATOM_DEV // 2, ATOM_DEV, 2).astype(jnp.int32),
        "shape_functions": gaussian(splits[5], (NSPEC, NL, BOX * BOX * BOX), (296.0 / BOX ** 1.5), 28.0, (), jnp.float32),
        "coupling": gaussian(splits[6], (NSPEC, NL, NI * NI), NL ** -0.5, 1.25, (), jnp.float32),
        "coulomb": gaussian(splits[7], (NSPEC, NI * NI, NI * NI), (NI * NI) ** -0.5, 0.375, (), jnp.float32),
        "rho_ij": gaussian(splits[8], (ATOMS, NI * NI), 1.0, 6.0, ((0, 128),), jnp.float32),
        "projections": gaussian(splits[9], (ATOMS, NI, BANDS), 1.0, 6.0, ((0, 128), (2, 4)), jnp.float32),
    }


GRID_H = 0.15
KAPPA = 0.804
MU_COEF = 0.2195149727645171
PRECISE = lax.Precision.HIGHEST

def exchange_energy(dens, sigma):
    prefactor = -0.75 * (3.0 / jnp.pi) ** (1.0 / 3.0)
    reduced = sigma / (4.0 * (3.0 * jnp.pi ** 2) ** (2.0 / 3.0) * dens ** (8.0 / 3.0))
    enhance = 1.0 + KAPPA - KAPPA / (1.0 + MU_COEF * reduced / KAPPA)
    return prefactor * dens ** (4.0 / 3.0) * enhance

def energy_slopes(dens, sigma):

    def summed(dens_in, sigma_in):
        return jnp.sum(exchange_energy(dens_in, sigma_in))
    return jax.grad(summed, argnums=(0, 1))(dens, sigma)

def hamiltonian_blocks(moments, rho_rows, picks, live, coupling, coulomb):
    summed = jnp.zeros((moments.shape[0], coulomb.shape[2]), moments.dtype)
    for spec_id in range(coupling.shape[0]):
        term = jnp.dot(moments, coupling[spec_id], precision=PRECISE) + 2.0 * jnp.dot(rho_rows, coulomb[spec_id], precision=PRECISE)
        summed = summed + picks[:, spec_id:spec_id + 1] * term
    return jnp.where(live[:, None], summed, 0.0)

def reference(density, hartree, box_root, species, atom_count, shape_functions, coupling, coulomb, rho_ij, projections):
    half_step = 0.5 / GRID_H
    grads = [(jnp.roll(density, -1, axis_dim) - jnp.roll(density, 1, axis_dim)) * half_step for axis_dim in range(3)]
    sigma = grads[0] * grads[0] + grads[1] * grads[1] + grads[2] * grads[2]
    slope_n, slope_s = energy_slopes(density, sigma)
    spread = jnp.zeros_like(density)
    for axis_dim in range(3):
        flux = slope_s * grads[axis_dim]
        spread = spread + (jnp.roll(flux, -1, axis_dim) - jnp.roll(flux, 1, axis_dim)) * half_step
    potential = hartree + slope_n - 2.0 * spread
    flat_shapes = shape_functions.reshape(NSPEC * NL, BOX * BOX * BOX)
    box_steps = jnp.arange(BOX, dtype=jnp.int32)
    spec_ids = jnp.arange(NSPEC, dtype=jnp.int32)

    def one_atom(inputs):
        root, species_id = inputs
        index_x = ((root[0] + box_steps) % NX).astype(jnp.int32)
        index_y = ((root[1] + box_steps) % NY).astype(jnp.int32)
        index_z = ((root[2] + box_steps) % NZ).astype(jnp.int32)
        window = potential[index_x][:, index_y][:, :, index_z].reshape(BOX * BOX * BOX)
        every = jnp.dot(flat_shapes, window, precision=PRECISE).reshape(NSPEC, NL)
        picks = (spec_ids == species_id).astype(every.dtype)
        return lax.optimization_barrier(jnp.sum(every * picks[:, None], axis=0)) * GRID_H ** 3
    moments = lax.map(one_atom, (box_root.T, species))
    slots = jnp.arange(ATOMS, dtype=jnp.int32)
    column = (slots // ATOM_DEV).astype(jnp.int32)
    live = slots % ATOM_DEV < atom_count[column]
    picks = (species[:, None] == spec_ids[None, :]).astype(moments.dtype)
    atom_hamiltonian = hamiltonian_blocks(moments, rho_ij, picks, live, coupling, coulomb)
    blocks = atom_hamiltonian.reshape(ATOMS, NI, NI)
    applied = jnp.einsum('aij,ajn->ain', blocks, projections, precision=PRECISE)
    return (potential, atom_hamiltonian, applied)
```

```python
import math

import jax
import jax.numpy as jnp
from jax import lax
from jax.experimental import pallas as pl
from jax.experimental.pallas import tpu as pltpu
from jax.sharding import PartitionSpec as P

BOX = 16
NI = 16
NL = 25
GRID_H = 0.15
HALF = 0.5 / GRID_H
KAPPA = 0.804
MU = 0.2195149727645171
A0 = -0.75 * (3.0 / math.pi) ** (1.0 / 3.0)
C0 = 4.0 * (3.0 * math.pi**2) ** (2.0 / 3.0)

CX, CY, CZ = 32, 24, 128
LOW = 2
DUP = 17
HUP = 15
XD = 56
XH = 48
YD = CY + LOW + DUP
YH = CY + HUP
F32, BF16 = jnp.float32, jnp.bfloat16
PARAMS = pltpu.CompilerParams(vmem_limit_bytes=48 * 1024 * 1024)


def shifted(block, axis, distance):
    n = lax.axis_size(axis)
    return lax.ppermute(block, axis, [(i, (i + distance) % n) for i in range(n)])


def split(value):
    high = value.astype(BF16)
    low = (value - high.astype(F32)).astype(BF16)
    return high, low


def dot(left, right):
    return jnp.dot(left, right, preferred_element_type=F32)


def dot3(left, right):
    lh, ll = split(left)
    rh, rl = split(right)
    return dot(lh, rh) + (dot(ll, rh) + dot(lh, rl))


def prep_kernel(shape_ref, rho_ref, coulomb_ref, pick_ref, shaped_ref, base_ref):
    pad = jnp.zeros((7, 128), F32)
    rest = jnp.zeros((64, 128), F32)
    for c in range(32):
        cols = pl.ds(c * 128, 128)
        rows = jnp.concatenate([shape_ref[0, :, cols], pad, shape_ref[1, :, cols], pad, rest], axis=0)
        turned = rows.T
        high = turned.astype(BF16).astype(F32)
        low = (turned - high).astype(BF16).astype(F32)
        shaped_ref[cols, :] = (high + pltpu.roll(low, 64, 1)).astype(BF16)
    rho = rho_ref[...]
    total = jnp.zeros((64, 256), F32)
    for s in range(2):
        total = total + dot3(rho * pick_ref[:, s : s + 1], coulomb_ref[s])
    base_ref[...] = 2.0 * total


def widen_kernel(dens_ref, hart_ref, above_ref, below_ref, ed_ref, eh_ref, down_ref, up_ref):
    ones = jnp.ones((CY, CZ), F32)
    for s in range(XD):
        x = s - LOW
        if x < 0:
            plane = below_ref[s]
        elif x < CX:
            plane = dens_ref[x]
        elif x < CX + DUP:
            plane = above_ref[x - CX]
        else:
            plane = ones
        ed_ref[pl.ds(s, CY, stride=XD), :] = plane
    for x in range(XH):
        if x < CX:
            plane = hart_ref[x]
        elif x < CX + HUP:
            plane = above_ref[DUP + x - CX]
        else:
            plane = ones
        eh_ref[pl.ds(x, CY, stride=XH), :] = plane
    down_ref[: DUP * XD] = ed_ref[: DUP * XD]
    down_ref[DUP * XD :] = eh_ref[: HUP * XH]
    up_ref[...] = ed_ref[(CY - LOW) * XD :]


def gather_density(ed_ref, down_ref, up_ref, dens, sems):
    copies = [
        pltpu.make_async_copy(up_ref, dens.at[pl.ds(0, LOW * XD)], sems.at[0]),
        pltpu.make_async_copy(ed_ref, dens.at[pl.ds(LOW * XD, CY * XD)], sems.at[1]),
        pltpu.make_async_copy(
            down_ref.at[pl.ds(0, DUP * XD)], dens.at[pl.ds((LOW + CY) * XD, DUP * XD)], sems.at[2]
        ),
    ]
    return copies


def ends_kernel(ed_ref, down_ref, up_ref, low_ref, high_ref, dens, sems):
    copies = gather_density(ed_ref, down_ref, up_ref, dens, sems)
    for copy in copies:
        copy.start()
    for copy in copies:
        copy.wait()
    lane = lax.broadcasted_iota(jnp.int32, (XD, 128), 1)

    def step(line, planes):
        rows = dens[pl.ds(pl.multiple_of(line * XD, 8), XD), :]
        here = lane == line
        return tuple(
            jnp.where(here, pltpu.roll(rows, lax.rem(line - z + 128, 128), 1), plane)
            for z, plane in zip((0, 1, 126, 127), planes)
        )

    start = jnp.ones((XD, 128), F32)
    planes = lax.fori_loop(0, YD, step, (start,) * 4)
    low_ref[:XD], low_ref[XD:] = planes[0], planes[1]
    high_ref[:XD], high_ref[XD:] = planes[2], planes[3]


def slopes(dens, sigma):
    root = jnp.exp(jnp.log(dens) * (1.0 / 3.0))
    inv = 1.0 / (dens * root)
    scaled = sigma * inv * inv
    t = 1.0 / (1.0 + (MU / (KAPPA * C0)) * scaled)
    tt = t * t
    slope_s = (A0 * MU / C0) * inv * tt
    slope_n = root * (
        (A0 * 4.0 / 3.0 * (1.0 + KAPPA) - (A0 * 4.0 / 3.0 * KAPPA) * t)
        - (A0 * 8.0 / 3.0 * MU / C0) * scaled * tt
    )
    return slope_n, slope_s


def field_kernel(
    plan_ref,
    ed_ref, eh_ref, down_ref, up_ref,
    low_ref, high_ref, after_ref, before_ref,
    shaped_ref, mask_ref,
    out_ref, part_ref,
    dens, hart, ends, flux_x, flux_y, local_n, field, windows, sems,
):
    copies = gather_density(ed_ref, down_ref, up_ref, dens, sems)
    copies += [
        pltpu.make_async_copy(eh_ref, hart.at[pl.ds(0, CY * XH)], sems.at[3]),
        pltpu.make_async_copy(
            down_ref.at[pl.ds(DUP * XD, HUP * XH)], hart.at[pl.ds(CY * XH, HUP * XH)], sems.at[4]
        ),
    ]
    for copy in copies:
        copy.start()
    windows[...] = jnp.zeros_like(windows)

    def outside(center, toward_high, toward_low):
        gx = (pltpu.roll(center, XD - 1, 0) - pltpu.roll(center, 1, 0)) * HALF
        gy = (pltpu.roll(center, 127, 1) - pltpu.roll(center, 1, 1)) * HALF
        gz = (toward_high - toward_low) * HALF
        _, slope_s = slopes(center, gx * gx + gy * gy + gz * gz)
        return slope_s * gz

    below = before_ref[XD:]
    above = after_ref[:XD]
    ends[0] = below
    ends[1] = above
    ends[2] = outside(below, low_ref[:XD], before_ref[:XD])
    ends[3] = outside(above, after_ref[XD:], high_ref[XD:])
    for copy in copies:
        copy.wait()

    lane = lax.broadcasted_iota(jnp.int32, (XD, 128), 1)
    first, last = lane == 0, lane == 127

    def z_pair(rows, low_end, high_end, line):
        up = jnp.where(last, pltpu.roll(high_end, 127 - line, 1), pltpu.roll(rows, 127, 1))
        down = jnp.where(first, pltpu.roll(low_end, 128 - line, 1), pltpu.roll(rows, 1, 1))
        return up - down

    def flux_step(line, carry):
        base = pl.multiple_of(line * XD, 8)
        center = dens[pl.ds(base, XD), :]
        gx = (dens[pl.ds(base + 1, XD), :] - dens[pl.ds(base - 1, XD), :]) * HALF
        gy = (
            dens[pl.ds(pl.multiple_of(base + XD, 8), XD), :]
            - dens[pl.ds(pl.multiple_of(base - XD, 8), XD), :]
        ) * HALF
        gz = z_pair(center, ends[0], ends[1], line) * HALF
        slope_n, slope_s = slopes(center, gx * gx + gy * gy + gz * gz)
        flux_x[pl.ds(base, XD), :] = slope_s * gx
        flux_y[pl.ds(base, XD), :] = slope_s * gy
        spread = z_pair(slope_s * gz, ends[2], ends[3], line)
        local_n[pl.ds(base, XD), :] = slope_n - (2.0 * HALF) * spread
        return carry

    lax.fori_loop(1, YD - 1, flux_step, 0)

    def field_step(y, carry):
        base = (y + LOW) * XD + LOW
        spread = (flux_x[pl.ds(base + 1, XH), :] - flux_x[pl.ds(base - 1, XH), :]) + (
            flux_y[pl.ds(base + XD, XH), :] - flux_y[pl.ds(base - XD, XH), :]
        )
        here = pl.multiple_of(y * XH, 8)
        value = hart[pl.ds(here, XH), :] + local_n[pl.ds(base, XH), :] - (2.0 * HALF) * spread
        field[pl.ds(here, XH), :] = value

        @pl.when(y < CY)
        def _():
            out_ref[pl.ds(y, CX, stride=CY), :] = value[:CX]

        return carry

    lax.fori_loop(0, YH, field_step, 0)

    step_z = lax.broadcasted_iota(jnp.int32, (16, 128), 1)
    group = step_z // 16
    step_z = step_z % 16

    def atom_step(atom, carry):
        @pl.when(plan_ref[3, atom] != 0)
        def _():
            rx, ry, rz = plan_ref[0, atom], plan_ref[1, atom], plan_ref[2, atom]
            shift = 128 - lax.rem(rz, 128)
            inside = ((step_z + rz) & 511) < 128
            for jh in range(2):
                packed = jnp.zeros((16, 128), F32)
                for jl in range(8):
                    j = jh * 8 + jl
                    rows = field[pl.ds((ry + j) * XH + rx, 16), :]
                    turned = pltpu.roll(rows, lax.rem(shift + jl * 16, 128), 1)
                    packed = jnp.where(group == jl, turned, packed)
                packed = jnp.where(inside, packed, 0.0)
                windows[pl.ds(atom + jh * 1024, 16, stride=64), :] = packed

        return carry

    lax.fori_loop(0, 64, atom_step, 0)

    total = jnp.zeros((128, 128), F32)
    for i in range(16):
        rows = [windows[pl.ds(jh * 1024 + i * 64, 64), :] for jh in range(2)]
        high, low = split(jnp.concatenate(rows, axis=1))
        both = jnp.concatenate([high, low], axis=0)
        total = total + dot(both, shaped_ref[pl.ds(i * 256, 256), :])
    total = total[:64] + total[64:]
    total = (total + pltpu.roll(total, 64, 1)) * mask_ref[...]
    for b in range(4):
        part_ref[b] = total


def apply_kernel(parts_ref, coupling_ref, base_ref, live_ref, proj_ref, ham_ref, out_ref, spread_ref):
    moments = (parts_ref[0] + parts_ref[1]) + (parts_ref[2] + parts_ref[3])
    ham = (dot3(moments, coupling_ref[...]) + base_ref[...]) * live_ref[:, :1]
    ham_ref[...] = ham
    lane = lax.broadcasted_iota(jnp.int32, (64, 128), 1)
    row = lax.broadcasted_iota(jnp.int32, (64, 128), 0)
    mine = (lane // 16) == (row % 8)
    halves = [pltpu.roll(ham[:, s : s + 128], 0, 1, stride=16, stride_axis=0) for s in (0, 128)]
    for i in range(16):
        placed = halves[i // 8]
        if i % 8:
            placed = pltpu.roll(placed, 128 - (i % 8) * 16, 1)
        spread_ref[pl.ds(i, 64, stride=16), :] = jnp.where(mine, placed, 0.0)
    for g in range(8):
        rows = pl.ds(g * 128, 128)
        out_ref[rows, :] = dot3(spread_ref[rows, :], proj_ref[rows, :])


def vmem(count):
    return [pl.BlockSpec(memory_space=pltpu.VMEM)] * count


def anywhere(count):
    return [pl.BlockSpec(memory_space=pl.ANY)] * count


def shape(*dims, dtype=F32):
    return jax.ShapeDtypeStruct(dims, dtype)


def local(
    density, hartree, box_root, species, atom_count, shape_functions, coupling, coulomb, rho_ij, projections
):
    slots = box_root.shape[1]
    first_x = lax.axis_index("dx") * CX
    first_y = lax.axis_index("dyz") * CY
    first_z = lax.axis_index("band") * CZ
    depth = CZ * lax.axis_size("band")

    above = shifted(jnp.concatenate([density[:DUP], hartree[:HUP]], axis=0), "dx", -1)
    below = shifted(density[CX - LOW :], "dx", 1)

    live = jnp.arange(slots, dtype=jnp.int32) < atom_count[0]
    offset = (box_root[2] - first_z) % depth
    meets = live & ((offset < CZ) | (offset > depth - BOX))
    plan = jnp.stack([box_root[0] - first_x, box_root[1] - first_y, offset, meets.astype(jnp.int32)])
    spec_lane = jnp.arange(128, dtype=jnp.int32)[None, :] // 32
    mask = (spec_lane == species[:, None]).astype(F32) * GRID_H**3
    picks = (jnp.arange(128, dtype=jnp.int32)[None, :] == species[:, None]).astype(F32)
    live_rows = jnp.broadcast_to(live[:, None], (slots, 128)).astype(F32)
    tensors = jnp.pad(coupling, ((0, 2), (0, 32 - NL), (0, 0))).reshape(128, NI * NI)

    shaped, base = pl.pallas_call(
        prep_kernel,
        out_shape=(shape(4096, 128, dtype=BF16), shape(64, 256)),
        in_specs=vmem(4),
        out_specs=tuple(vmem(2)),
        compiler_params=PARAMS,
        name="prep",
    )(shape_functions, rho_ij, coulomb, picks)

    wide_d, wide_h, send_down, send_up = pl.pallas_call(
        widen_kernel,
        out_shape=(
            shape(CY * XD, CZ),
            shape(CY * XH, CZ),
            shape(DUP * XD + HUP * XH, CZ),
            shape(LOW * XD, CZ),
        ),
        in_specs=vmem(4),
        out_specs=tuple(vmem(4)),
        compiler_params=PARAMS,
        name="widen",
    )(density, hartree, above, below)

    from_up = shifted(send_down, "dyz", -1)
    from_down = shifted(send_up, "dyz", 1)

    low, high = pl.pallas_call(
        ends_kernel,
        out_shape=(shape(2 * XD, 128), shape(2 * XD, 128)),
        in_specs=anywhere(3),
        out_specs=tuple(vmem(2)),
        scratch_shapes=[pltpu.VMEM((YD * XD, CZ), F32), pltpu.SemaphoreType.DMA((3,))],
        compiler_params=PARAMS,
        name="ends",
    )(wide_d, from_up, from_down)

    after = shifted(low, "band", -1)
    before = shifted(high, "band", 1)

    potential, parts = pl.pallas_call(
        field_kernel,
        out_shape=(shape(CX * CY, CZ), shape(4, 64, 128)),
        in_specs=[pl.BlockSpec(memory_space=pltpu.SMEM)] + anywhere(4) + vmem(6),
        out_specs=tuple(vmem(2)),
        scratch_shapes=[
            pltpu.VMEM((YD * XD, CZ), F32),
            pltpu.VMEM((YH * XH, CZ), F32),
            pltpu.VMEM((4, XD, 128), F32),
            pltpu.VMEM((YD * XD, CZ), F32),
            pltpu.VMEM((YD * XD, CZ), F32),
            pltpu.VMEM((YD * XD, CZ), F32),
            pltpu.VMEM((YH * XH, CZ), F32),
            pltpu.VMEM((2 * 16 * 64, 128), F32),
            pltpu.SemaphoreType.DMA((5,)),
        ],
        compiler_params=PARAMS,
        name="field",
    )(plan, wide_d, wide_h, from_up, from_down, low, high, after, before, shaped, mask)

    parts = lax.all_to_all(parts, "band", 0, 0)

    atom_hamiltonian, applied = pl.pallas_call(
        apply_kernel,
        out_shape=(shape(64, 256), shape(64 * NI, 128)),
        in_specs=vmem(5),
        out_specs=tuple(vmem(2)),
        scratch_shapes=[pltpu.VMEM((64 * NI, 128), F32)],
        compiler_params=PARAMS,
        name="apply",
    )(parts, tensors, base, live_rows, projections.reshape(slots * NI, CZ))
    return (
        potential.reshape(CX, CY, CZ),
        atom_hamiltonian,
        applied.reshape(slots, NI, CZ),
    )


def solution(mesh):
    in_specs = (
        P("dx", "dyz", "band"),
        P("dx", "dyz", "band"),
        P(None, ("dx", "dyz")),
        P(("dx", "dyz")),
        P(("dx", "dyz")),
        P(),
        P(),
        P(),
        P(("dx", "dyz"), None),
        P(("dx", "dyz"), None, "band"),
    )
    out_specs = (P("dx", "dyz", "band"), P(("dx", "dyz"), None), P(("dx", "dyz"), None, "band"))
    return jax.shard_map(local, mesh=mesh, in_specs=in_specs, out_specs=out_specs, check_vma=False)
```

```python
import math

import jax
import jax.numpy as jnp
from jax import lax
from jax.experimental import pallas as pl
from jax.experimental.pallas import tpu as pltpu
from jax.sharding import PartitionSpec as P

BOX = 16
NI = 16
NL = 25
GRID_H = 0.15
HALF = 0.5 / GRID_H
KAPPA = 0.804
MU = 0.2195149727645171
A0 = -0.75 * (3.0 / math.pi) ** (1.0 / 3.0)
C0 = 4.0 * (3.0 * math.pi**2) ** (2.0 / 3.0)

CX, CY, CZ = 32, 24, 128
LOW = 2
DUP = 17
HUP = 15
XD = 56
XH = 48
YD = CY + LOW + DUP
YH = CY + HUP
F32, BF16 = jnp.float32, jnp.bfloat16
PARAMS = pltpu.CompilerParams(vmem_limit_bytes=16 * 1024 * 1024)


def shifted(block, axis, distance):
    n = lax.axis_size(axis)
    return lax.ppermute(block, axis, [(i, (i + distance) % n) for i in range(n)])


def split(value):
    high = value.astype(BF16)
    low = (value - high.astype(F32)).astype(BF16)
    return high, low


def dot(left, right):
    return jnp.dot(left, right, preferred_element_type=F32)


def dot3(left, right):
    lh, ll = split(left)
    rh, rl = split(right)
    return dot(lh, rh) + (dot(ll, rh) + dot(lh, rl))


def prep_kernel(shape_ref, rho_ref, coulomb_ref, pick_ref, shaped_ref, base_ref):
    pad = jnp.zeros((7, 128), F32)
    rest = jnp.zeros((64, 128), F32)
    for c in range(32):
        cols = pl.ds(c * 128, 128)
        rows = jnp.concatenate([shape_ref[0, :, cols], pad, shape_ref[1, :, cols], pad, rest], axis=0)
        turned = rows.T
        high = turned.astype(BF16).astype(F32)
        low = (turned - high).astype(BF16).astype(F32)
        shaped_ref[cols, :] = (high + pltpu.roll(low, 64, 1)).astype(BF16)
    rho = rho_ref[...]
    total = jnp.zeros((64, 256), F32)
    for s in range(2):
        total = total + dot3(rho * pick_ref[:, s : s + 1], coulomb_ref[s])
    base_ref[...] = 2.0 * total


def widen_kernel(dens_ref, hart_ref, above_ref, below_ref, ed_ref, eh_ref, down_ref, up_ref):
    ones = jnp.ones((CY, CZ), F32)
    for s in range(XD):
        x = s - LOW
        if x < 0:
            plane = below_ref[s]
        elif x < CX:
            plane = dens_ref[x]
        elif x < CX + DUP:
            plane = above_ref[x - CX]
        else:
            plane = ones
        ed_ref[pl.ds(s, CY, stride=XD), :] = plane
    for x in range(XH):
        if x < CX:
            plane = hart_ref[x]
        elif x < CX + HUP:
            plane = above_ref[DUP + x - CX]
        else:
            plane = ones
        eh_ref[pl.ds(x, CY, stride=XH), :] = plane
    down_ref[: DUP * XD] = ed_ref[: DUP * XD]
    down_ref[DUP * XD :] = eh_ref[: HUP * XH]
    up_ref[...] = ed_ref[(CY - LOW) * XD :]


def packed(own, tile, lines, group):
    for line, rows in lines:
        if line // 32 == tile:
            turned = pltpu.roll(rows, (4 * (line % 32) + 2) % 128, 1)
            own = jnp.where(group == line % 32, turned, own)
    return own


def line_group():
    return lax.broadcasted_iota(jnp.int32, (XD, 128), 1) // 4


def ends_kernel(own_ref, down_ref, up_ref, ends_ref):
    group = line_group()
    lines = [(0, up_ref[:XD]), (1, up_ref[XD:])]
    lines += [(LOW + CY + i, down_ref[i * XD : (i + 1) * XD]) for i in range(DUP)]
    for tile in range(2):
        cols = pl.ds(tile * 128, 128)
        ends_ref[:, cols] = packed(own_ref[:, cols], tile, lines, group)


def slopes(dens, sigma):
    root = jnp.exp(jnp.log(dens) * (1.0 / 3.0))
    inv = 1.0 / (dens * root)
    scaled = sigma * inv * inv
    t = 1.0 / (1.0 + (MU / (KAPPA * C0)) * scaled)
    tt = t * t
    slope_s = (A0 * MU / C0) * inv * tt
    slope_n = root * (
        (A0 * 4.0 / 3.0 * (1.0 + KAPPA) - (A0 * 4.0 / 3.0 * KAPPA) * t)
        - (A0 * 8.0 / 3.0 * MU / C0) * scaled * tt
    )
    return slope_n, slope_s


def line_flux(center, x_up, x_down, y_up, y_down):
    gx = (x_up - x_down) * HALF
    gy = (y_up - y_down) * HALF
    gz = (pltpu.roll(center, 127, 1) - pltpu.roll(center, 1, 1)) * HALF
    slope_n, slope_s = slopes(center, gx * gx + gy * gy + gz * gz)
    fx, fy, fz = slope_s * gx, slope_s * gy, slope_s * gz
    spread = (pltpu.roll(fx, XD - 1, 0) - pltpu.roll(fx, 1, 0)) + (
        pltpu.roll(fz, 127, 1) - pltpu.roll(fz, 1, 1)
    )
    return slope_n - (2.0 * HALF) * spread, fy


def flux_lines(source, first, count, local_ref, flux_ref, target):
    def step(i, carry):
        base = pl.multiple_of((first + i) * XD, 8)
        goal = pl.ds(pl.multiple_of((target + i) * XD, 8), XD)
        part, flux = line_flux(
            source[pl.ds(base, XD), :],
            source[pl.ds(base + 1, XD), :],
            source[pl.ds(base - 1, XD), :],
            source[pl.ds(pl.multiple_of(base + XD, 8), XD), :],
            source[pl.ds(pl.multiple_of(base - XD, 8), XD), :],
        )
        local_ref[goal, :] = part
        flux_ref[goal, :] = flux
        return carry

    lax.fori_loop(0, count, step, 0, unroll=2)


def inner_kernel(ed_ref, local_ref, flux_ref, ends_ref):
    group = line_group()
    lines = [(LOW + i, ed_ref[i * XD : (i + 1) * XD]) for i in range(CY)]
    for tile in range(2):
        ends_ref[:, pl.ds(tile * 128, 128)] = packed(jnp.ones((XD, 128), F32), tile, lines, group)
    flux_lines(ed_ref, 1, CY - 2, local_ref, flux_ref, 0)


def packed_flux(dens):
    gx = (pltpu.roll(dens, XD - 1, 0) - pltpu.roll(dens, 1, 0)) * HALF
    gy = (pltpu.roll(dens, 252, 1) - pltpu.roll(dens, 4, 1)) * HALF
    gz = (pltpu.roll(dens, 255, 1) - pltpu.roll(dens, 1, 1)) * HALF
    slope_n, slope_s = slopes(dens, gx * gx + gy * gy + gz * gz)
    return slope_n, slope_s * gx, slope_s * gy, slope_s * gz


def outer_kernel(ed_ref, down_ref, up_ref, ends_ref, local1_ref, flux1_ref, bulk_ref, wrap_ref, near, far, part, flux):
    near[: 2 * XD] = up_ref[...]
    near[2 * XD :] = ed_ref[: 2 * XD]
    far[: 2 * XD] = ed_ref[(CY - 2) * XD :]
    far[2 * XD :] = down_ref[: DUP * XD]
    mine = pl.ds(3 * XD, (CY - 2) * XD)
    part[mine, :] = local1_ref[...]
    flux[mine, :] = flux1_ref[...]
    flux_lines(near, 1, 2, part, flux, 1)
    flux_lines(far, 1, DUP, part, flux, CY + 1)

    def step(y, carry):
        base = (y + LOW) * XD + LOW
        spread = flux[pl.ds(base + XD, XH), :] - flux[pl.ds(base - XD, XH), :]
        bulk_ref[pl.ds(pl.multiple_of(y * XH, 8), XH), :] = part[pl.ds(base, XH), :] - (2.0 * HALF) * spread
        return carry

    lax.fori_loop(0, YH, step, 0, unroll=3)
    for i, value in enumerate(packed_flux(ends_ref[...])):
        wrap_ref[i] = value


def field_kernel(
    plan_ref,
    bulk_ref, eh_ref, down_ref, ends_ref, after_ref, before_ref, wrap_ref,
    shaped_ref, mask_ref,
    out_ref, part_ref,
    field, windows, fixes,
):
    windows[...] = jnp.zeros_like(windows)
    place = lax.broadcasted_iota(jnp.int32, (XD, 256), 1) % 4
    middle = (place == 1) | (place == 2)
    low = place < 2
    own = ends_ref[...]

    def fix(dens):
        dn, dx, dy, dz = [
            jnp.where(middle, value - wrap_ref[i], 0.0) for i, value in enumerate(packed_flux(dens))
        ]
        spread = (
            (pltpu.roll(dx, XD - 1, 0) - pltpu.roll(dx, 1, 0))
            + (pltpu.roll(dy, 252, 1) - pltpu.roll(dy, 4, 1))
            + (pltpu.roll(dz, 255, 1) - pltpu.roll(dz, 1, 1))
        )
        return dn - (2.0 * HALF) * spread

    top = fix(jnp.where(low, own, after_ref[...]))
    bottom = fix(jnp.where(low, before_ref[...], own))
    fixes[...] = jnp.where(low, top, bottom)

    lane = lax.broadcasted_iota(jnp.int32, (XH, 128), 1)
    edge = (lane < 2) | (lane >= 126)
    tiles = [fixes[pl.ds(LOW, XH), pl.ds(t * 128, 128)] for t in range(2)]

    for y in range(YH):
        line = y + LOW
        turned = pltpu.roll(tiles[line // 32], (254 - 4 * (line % 32)) % 128, 1)
        rows = pl.ds(y * XH, XH)
        hart = eh_ref[rows, :] if y < CY else down_ref[pl.ds(DUP * XD + (y - CY) * XH, XH), :]
        value = (hart + bulk_ref[rows, :]) + jnp.where(edge, turned, 0.0)
        field[rows, :] = value
        if y < CY:
            out_ref[pl.ds(y, CX, stride=CY), :] = value[:CX]

    step_z = lax.broadcasted_iota(jnp.int32, (16, 128), 1)
    group = step_z // 16
    step_z = step_z % 16

    def atom_step(atom, carry):
        @pl.when(plan_ref[3, atom] != 0)
        def _():
            rx, ry, rz = plan_ref[0, atom], plan_ref[1, atom], plan_ref[2, atom]
            shift = 128 - lax.rem(rz, 128)
            inside = ((step_z + rz) & 511) < 128
            for jh in range(2):
                packed = jnp.zeros((16, 128), F32)
                for jl in range(8):
                    j = jh * 8 + jl
                    rows = field[pl.ds((ry + j) * XH + rx, 16), :]
                    turned = pltpu.roll(rows, lax.rem(shift + jl * 16, 128), 1)
                    packed = jnp.where(group == jl, turned, packed)
                packed = jnp.where(inside, packed, 0.0)
                windows[pl.ds(atom + jh * 1024, 16, stride=64), :] = packed

        return carry

    lax.fori_loop(0, 64, atom_step, 0)

    total = jnp.zeros((128, 128), F32)
    for i in range(16):
        rows = [windows[pl.ds(jh * 1024 + i * 64, 64), :] for jh in range(2)]
        high, low = split(jnp.concatenate(rows, axis=1))
        both = jnp.concatenate([high, low], axis=0)
        total = total + dot(both, shaped_ref[pl.ds(i * 256, 256), :])
    total = total[:64] + total[64:]
    total = (total + pltpu.roll(total, 64, 1)) * mask_ref[...]
    for b in range(4):
        part_ref[b] = total


def apply_kernel(parts_ref, coupling_ref, base_ref, live_ref, proj_ref, ham_ref, out_ref, spread_ref):
    moments = (parts_ref[0] + parts_ref[1]) + (parts_ref[2] + parts_ref[3])
    ham = (dot3(moments, coupling_ref[...]) + base_ref[...]) * live_ref[:, :1]
    ham_ref[...] = ham
    lane = lax.broadcasted_iota(jnp.int32, (64, 128), 1)
    row = lax.broadcasted_iota(jnp.int32, (64, 128), 0)
    mine = (lane // 16) == (row % 8)
    halves = [pltpu.roll(ham[:, s : s + 128], 0, 1, stride=16, stride_axis=0) for s in (0, 128)]
    for i in range(16):
        placed = halves[i // 8]
        if i % 8:
            placed = pltpu.roll(placed, 128 - (i % 8) * 16, 1)
        spread_ref[pl.ds(i, 64, stride=16), :] = jnp.where(mine, placed, 0.0)
    for g in range(8):
        rows = pl.ds(g * 128, 128)
        out_ref[rows, :] = dot3(spread_ref[rows, :], proj_ref[rows, :])


def vmem(count):
    return [pl.BlockSpec(memory_space=pltpu.VMEM)] * count


def shape(*dims, dtype=F32):
    return jax.ShapeDtypeStruct(dims, dtype)


def local(
    density, hartree, box_root, species, atom_count, shape_functions, coupling, coulomb, rho_ij, projections
):
    slots = box_root.shape[1]
    first_x = lax.axis_index("dx") * CX
    first_y = lax.axis_index("dyz") * CY
    first_z = lax.axis_index("band") * CZ
    depth = CZ * lax.axis_size("band")

    above = shifted(jnp.concatenate([density[:DUP], hartree[:HUP]], axis=0), "dx", -1)
    below = shifted(density[CX - LOW :], "dx", 1)

    live = jnp.arange(slots, dtype=jnp.int32) < atom_count[0]
    offset = (box_root[2] - first_z) % depth
    meets = live & ((offset < CZ) | (offset > depth - BOX))
    plan = jnp.stack([box_root[0] - first_x, box_root[1] - first_y, offset, meets.astype(jnp.int32)])
    spec_lane = jnp.arange(128, dtype=jnp.int32)[None, :] // 32
    mask = (spec_lane == species[:, None]).astype(F32) * GRID_H**3
    picks = (jnp.arange(128, dtype=jnp.int32)[None, :] == species[:, None]).astype(F32)
    live_rows = jnp.broadcast_to(live[:, None], (slots, 128)).astype(F32)
    tensors = jnp.pad(coupling, ((0, 2), (0, 32 - NL), (0, 0))).reshape(128, NI * NI)

    shaped, base = pl.pallas_call(
        prep_kernel,
        out_shape=(shape(4096, 128, dtype=BF16), shape(64, 256)),
        in_specs=vmem(4),
        out_specs=tuple(vmem(2)),
        compiler_params=PARAMS,
        name="prep",
    )(shape_functions, rho_ij, coulomb, picks)

    wide_d, wide_h, send_down, send_up = pl.pallas_call(
        widen_kernel,
        out_shape=(
            shape(CY * XD, CZ),
            shape(CY * XH, CZ),
            shape(DUP * XD + HUP * XH, CZ),
            shape(LOW * XD, CZ),
        ),
        in_specs=vmem(4),
        out_specs=tuple(vmem(4)),
        compiler_params=PARAMS,
        name="widen",
    )(density, hartree, above, below)

    from_up = shifted(send_down, "dyz", -1)
    from_down = shifted(send_up, "dyz", 1)

    local1, flux1, ends1 = pl.pallas_call(
        inner_kernel,
        out_shape=(shape((CY - 2) * XD, CZ), shape((CY - 2) * XD, CZ), shape(XD, 256)),
        in_specs=vmem(1),
        out_specs=tuple(vmem(3)),
        compiler_params=PARAMS,
        name="inner",
    )(wide_d)

    ends = pl.pallas_call(
        ends_kernel,
        out_shape=shape(XD, 256),
        in_specs=vmem(3),
        out_specs=vmem(1)[0],
        compiler_params=PARAMS,
        name="ends",
    )(ends1, from_up, from_down)

    after = shifted(ends, "band", -1)
    before = shifted(ends, "band", 1)

    bulk, wrap = pl.pallas_call(
        outer_kernel,
        out_shape=(shape(YH * XH, CZ), shape(4, XD, 256)),
        in_specs=vmem(6),
        out_specs=tuple(vmem(2)),
        scratch_shapes=[
            pltpu.VMEM((4 * XD, CZ), F32),
            pltpu.VMEM((19 * XD, CZ), F32),
            pltpu.VMEM((YD * XD, CZ), F32),
            pltpu.VMEM((YD * XD, CZ), F32),
        ],
        compiler_params=PARAMS,
        name="outer",
    )(wide_d, from_up, from_down, ends, local1, flux1)

    potential, parts = pl.pallas_call(
        field_kernel,
        out_shape=(shape(CX * CY, CZ), shape(4, 64, 128)),
        in_specs=[pl.BlockSpec(memory_space=pltpu.SMEM)] + vmem(9),
        out_specs=tuple(vmem(2)),
        scratch_shapes=[
            pltpu.VMEM((YH * XH, CZ), F32),
            pltpu.VMEM((2 * 16 * 64, 128), F32),
            pltpu.VMEM((XD, 256), F32),
        ],
        compiler_params=PARAMS,
        name="field",
    )(plan, bulk, wide_h, from_up, ends, after, before, wrap, shaped, mask)

    parts = lax.all_to_all(parts, "band", 0, 0)

    atom_hamiltonian, applied = pl.pallas_call(
        apply_kernel,
        out_shape=(shape(64, 256), shape(64 * NI, 128)),
        in_specs=vmem(5),
        out_specs=tuple(vmem(2)),
        scratch_shapes=[pltpu.VMEM((64 * NI, 128), F32)],
        compiler_params=PARAMS,
        name="apply",
    )(parts, tensors, base, live_rows, projections.reshape(slots * NI, CZ))
    return (
        potential.reshape(CX, CY, CZ),
        atom_hamiltonian,
        applied.reshape(slots, NI, CZ),
    )


def solution(mesh):
    in_specs = (
        P("dx", "dyz", "band"),
        P("dx", "dyz", "band"),
        P(None, ("dx", "dyz")),
        P(("dx", "dyz")),
        P(("dx", "dyz")),
        P(),
        P(),
        P(),
        P(("dx", "dyz"), None),
        P(("dx", "dyz"), None, "band"),
    )
    out_specs = (P("dx", "dyz", "band"), P(("dx", "dyz"), None), P(("dx", "dyz"), None, "band"))
    return jax.shard_map(local, mesh=mesh, in_specs=in_specs, out_specs=out_specs, check_vma=False)
```

```python
import math

import jax
import jax.numpy as jnp
from jax import lax
from jax.experimental import pallas as pl
from jax.experimental.pallas import tpu as pltpu
from jax.sharding import PartitionSpec as P

BOX = 16
NI = 16
NL = 25
GRID_H = 0.15
HALF = 0.5 / GRID_H
KAPPA = 0.804
MU = 0.2195149727645171
A0 = -0.75 * (3.0 / math.pi) ** (1.0 / 3.0)
C0 = 4.0 * (3.0 * math.pi**2) ** (2.0 / 3.0)

CX, CY, CZ = 32, 24, 128
LOW = 2
DUP = 17
HUP = 15
XD = 56
XH = 48
YD = CY + LOW + DUP
YH = CY + HUP
F32, BF16 = jnp.float32, jnp.bfloat16
PARAMS = pltpu.CompilerParams(vmem_limit_bytes=16 * 1024 * 1024)


def shifted(block, axis, distance):
    n = lax.axis_size(axis)
    return lax.ppermute(block, axis, [(i, (i + distance) % n) for i in range(n)])


def split(value):
    high = value.astype(BF16)
    low = (value - high.astype(F32)).astype(BF16)
    return high, low


def dot(left, right):
    return jnp.dot(left, right, preferred_element_type=F32)


def dot3(left, right):
    lh, ll = split(left)
    rh, rl = split(right)
    return dot(lh, rh) + (dot(ll, rh) + dot(lh, rl))


def column(row):
    shape = (64, 64)
    diagonal = lax.broadcasted_iota(jnp.int32, shape, 0) == lax.broadcasted_iota(jnp.int32, shape, 1)
    spread = jnp.broadcast_to(row.astype(F32), shape)
    return jnp.sum(jnp.where(diagonal, spread, 0.0), axis=1, keepdims=True)


def base_kernel(after_ref, rho_ref, coulomb_ref, kinds_ref, base_ref):
    rho = rho_ref[...]
    kind = kinds_ref[1, :, :1]
    total = jnp.zeros((64, 256), F32)
    for s in range(2):
        total = total + dot3(jnp.where(kind == s, rho, 0.0), coulomb_ref[s])
    base_ref[...] = 2.0 * total


def plan_kernel(root_ref, count_ref, rows_hbm, species_hbm, plan_ref, kinds_ref, rows_ref, species_ref, sems):
    copies = [
        pltpu.make_async_copy(rows_hbm, rows_ref, sems.at[0]),
        pltpu.make_async_copy(species_hbm, species_ref, sems.at[1]),
    ]
    for copy in copies:
        copy.start()
    first_z = lax.axis_index("band") * CZ
    count = count_ref[0]

    def step(i, found):
        for atom in [4 * i + k for k in range(4)]:
            offset = (root_ref[2, atom] - first_z) & 511
            meets = (atom < count) & ((offset < CZ) | (offset > 512 - BOX))
            plan_ref[found] = atom
            found = found + meets.astype(jnp.int32)
        return found

    plan_ref[65] = lax.fori_loop(0, (count + 3) // 4, step, 0)
    for copy in copies:
        copy.wait()
    offset = (rows_ref[2:3, :] - first_z) & 511
    live = lax.broadcasted_iota(jnp.int32, (1, 64), 1) < count_ref[0]
    meets = live & ((offset < CZ) | (offset > 512 - BOX))
    for i, here in enumerate((meets, live)):
        kinds_ref[i] = jnp.broadcast_to(column(jnp.where(here, species_ref[...], 2)), (64, 128))


def lift_kernel(dens_ref, hart_ref, low_ref, high_ref, hart_low_ref, sems):
    copies = [
        pltpu.make_async_copy(dens_ref.at[pl.ds(0, DUP)], low_ref, sems.at[0]),
        pltpu.make_async_copy(dens_ref.at[pl.ds(CX - LOW, LOW)], high_ref, sems.at[1]),
        pltpu.make_async_copy(hart_ref.at[:, pl.ds(0, 16), :], hart_low_ref, sems.at[2]),
    ]
    for copy in copies:
        copy.start()
    for copy in copies:
        copy.wait()


def widen_kernel(after_ref, dens_ref, above_ref, below_ref, ed_ref, down_ref, up_ref):
    for s in range(XD):
        x = s - LOW
        if x < 0:
            plane = below_ref[s]
        elif x < CX:
            plane = dens_ref[x]
        elif x < CX + DUP:
            plane = above_ref[x - CX]
        else:
            plane = jnp.ones((CY, CZ), F32)
        ed_ref[pl.ds(s, CY, stride=XD), :] = plane
    down_ref[...] = ed_ref[: DUP * XD]
    up_ref[...] = ed_ref[(CY - LOW) * XD :]


def turn_kernel(after1_ref, after2_ref, hart_ref, above_ref, send_ref):
    for x in range(16):
        send_ref[pl.ds(x, CY, stride=16), :] = hart_ref[x]
        send_ref[pl.ds(CY * 16 + x, 16, stride=16), :] = above_ref[x]


def packed(own, tile, lines, group):
    for line, rows in lines:
        if line // 32 == tile:
            turned = pltpu.roll(rows, (4 * (line % 32) + 2) % 128, 1)
            own = jnp.where(group == line % 32, turned, own)
    return own


def line_group():
    return lax.broadcasted_iota(jnp.int32, (XD, 128), 1) // 4


def ends_kernel(own_ref, down_ref, up_ref, ends_ref, send_ref):
    group = line_group()
    lines = [(0, up_ref[:XD]), (1, up_ref[XD:])]
    lines += [(LOW + CY + i, down_ref[i * XD : (i + 1) * XD]) for i in range(DUP)]
    tiles = []
    for tile in range(2):
        cols = pl.ds(tile * 128, 128)
        tiles.append(packed(own_ref[:, cols], tile, lines, group))
        ends_ref[:, cols] = tiles[tile]
    place = lax.broadcasted_iota(jnp.int32, (XD, 128), 1) % 4
    to_below = jnp.where(place >= 2, tiles[0], pltpu.roll(tiles[1], 126, 1))
    to_above = jnp.where(place < 2, tiles[0], pltpu.roll(tiles[1], 2, 1))
    below = (lax.axis_index("band") + 3) & 3
    for b in range(4):
        send_ref[b] = jnp.where(below == b, to_below, to_above)


def slopes(dens, sigma):
    power = jnp.log2(dens)
    root = jnp.exp2(power * (1.0 / 3.0))
    inv = jnp.exp2(power * (-4.0 / 3.0))
    scaled = sigma * (inv * inv)
    below = 1.0 + (MU / (KAPPA * C0)) * scaled
    t = pl.reciprocal(below, approx=True)
    t = t * (2.0 - below * t)
    tt = t * t
    slope_s = (A0 * MU / C0) * (inv * tt)
    slope_n = root * (
        (A0 * 4.0 / 3.0 * (1.0 + KAPPA) - (A0 * 4.0 / 3.0 * KAPPA) * t)
        - (A0 * 8.0 / 3.0 * MU / C0) * (scaled * tt)
    )
    return slope_n, slope_s


def line_flux(center, x_up, x_down, y_up, y_down):
    gx = (x_up - x_down) * HALF
    gy = (y_up - y_down) * HALF
    gz = (pltpu.roll(center, 127, 1) - pltpu.roll(center, 1, 1)) * HALF
    slope_n, slope_s = slopes(center, gx * gx + gy * gy + gz * gz)
    fx, fy, fz = slope_s * gx, slope_s * gy, slope_s * gz
    spread = (pltpu.roll(fx, XD - 1, 0) - pltpu.roll(fx, 1, 0)) + (
        pltpu.roll(fz, 127, 1) - pltpu.roll(fz, 1, 1)
    )
    return slope_n - (2.0 * HALF) * spread, fy


def flux_lines(source, first, count, local_ref, flux_ref, target):
    def step(i, carry):
        base = pl.multiple_of((first + i) * XD, 8)
        goal = pl.ds(pl.multiple_of((target + i) * XD, 8), XD)
        part, flux = line_flux(
            source[pl.ds(base, XD), :],
            source[pl.ds(base + 1, XD), :],
            source[pl.ds(base - 1, XD), :],
            source[pl.ds(pl.multiple_of(base + XD, 8), XD), :],
            source[pl.ds(pl.multiple_of(base - XD, 8), XD), :],
        )
        local_ref[goal, :] = part
        flux_ref[goal, :] = flux
        return carry

    lax.fori_loop(0, count, step, 0, unroll=2)


def packed_flux(dens):
    gx = (pltpu.roll(dens, XD - 1, 0) - pltpu.roll(dens, 1, 0)) * HALF
    gy = (pltpu.roll(dens, 252, 1) - pltpu.roll(dens, 4, 1)) * HALF
    gz = (pltpu.roll(dens, 255, 1) - pltpu.roll(dens, 1, 1)) * HALF
    slope_n, slope_s = slopes(dens, gx * gx + gy * gy + gz * gz)
    return slope_n, slope_s * gx, slope_s * gy, slope_s * gz


def bulk_lines(part, flux, first, count, bulk_ref):
    def step(i, carry):
        base = (first + i) * XD + LOW
        spread = flux[pl.ds(base + XD, XH), :] - flux[pl.ds(base - XD, XH), :]
        goal = pl.ds(pl.multiple_of(i * XH, 8), XH)
        bulk_ref[goal, :] = part[pl.ds(base, XH), :] - (2.0 * HALF) * spread
        return carry

    lax.fori_loop(0, count, step, 0, unroll=2)


def inner_kernel(ed_ref, bulk_ref, tail_ref, ends_ref, part, flux):
    group = line_group()
    lines = [(LOW + i, ed_ref[i * XD : (i + 1) * XD]) for i in range(CY)]
    for tile in range(2):
        ends_ref[:, pl.ds(tile * 128, 128)] = packed(jnp.ones((XD, 128), F32), tile, lines, group)
    flux_lines(ed_ref, 1, 22, part, flux, 0)
    bulk_lines(part, flux, 1, 20, bulk_ref)
    tail_ref[: 2 * XD] = flux[: 2 * XD]
    tail_ref[2 * XD : 4 * XD] = flux[20 * XD :]
    tail_ref[4 * XD : 5 * XD] = part[:XD]
    tail_ref[5 * XD : 6 * XD] = part[21 * XD :]
    tail_ref[6 * XD : 8 * XD] = ed_ref[: 2 * XD]
    tail_ref[8 * XD :] = ed_ref[22 * XD :]


def outer_kernel(down_ref, up_ref, tail_ref, ends_ref, bulk_ref, wrap_ref, near, near_part, near_flux, far, part, flux):
    near[: 2 * XD] = up_ref[...]
    near[2 * XD :] = tail_ref[6 * XD : 8 * XD]
    near_flux[2 * XD :] = tail_ref[: 2 * XD]
    near_part[2 * XD :] = tail_ref[4 * XD : 5 * XD]
    far[: 2 * XD] = tail_ref[8 * XD :]
    far[2 * XD :] = down_ref[...]
    flux[: 2 * XD] = tail_ref[2 * XD : 4 * XD]
    part[XD : 2 * XD] = tail_ref[5 * XD : 6 * XD]
    flux_lines(near, 1, 2, near_part, near_flux, 0)
    flux_lines(far, 1, DUP, part, flux, 2)
    bulk_lines(near_part, near_flux, 1, 2, bulk_ref.at[pl.ds(0, 2 * XH)])
    bulk_lines(part, flux, 1, DUP, bulk_ref.at[pl.ds(2 * XH, DUP * XH)])
    for i, value in enumerate(packed_flux(ends_ref[...])):
        wrap_ref[i] = value


def field_kernel(
    root_ref, plan_ref,
    hart_ref, cells_ref,
    hart_above, hart_right, bulk1_ref, bulk2_ref, ends_ref, beside_ref, wrap_ref, kinds_ref,
    field, part_ref,
    hart, cells, windows, fixes, sems,
):
    copies = [
        pltpu.make_async_copy(hart_ref, hart, sems.at[0]),
        pltpu.make_async_copy(cells_ref, cells, sems.at[1]),
    ]
    for copy in copies:
        copy.start()
    place = lax.broadcasted_iota(jnp.int32, (XD, 256), 1) % 4
    middle = (place == 1) | (place == 2)
    low = place < 2
    own = ends_ref[...]

    def fix(dens):
        dn, dx, dy, dz = [
            jnp.where(middle, value - wrap_ref[i], 0.0) for i, value in enumerate(packed_flux(dens))
        ]
        spread = (
            (pltpu.roll(dx, XD - 1, 0) - pltpu.roll(dx, 1, 0))
            + (pltpu.roll(dy, 252, 1) - pltpu.roll(dy, 4, 1))
            + (pltpu.roll(dz, 255, 1) - pltpu.roll(dz, 1, 1))
        )
        return dn - (2.0 * HALF) * spread

    band = lax.axis_index("band")
    after = beside_ref[(band + 1) & 3]
    before = beside_ref[(band + 3) & 3]
    after = jnp.concatenate([after, pltpu.roll(after, 2, 1)], axis=1)
    before = jnp.concatenate([before, pltpu.roll(before, 126, 1)], axis=1)
    top = fix(jnp.where(low, own, after))
    bottom = fix(jnp.where(low, before, own))
    fixes[...] = jnp.where(low, top, bottom)

    lane = lax.broadcasted_iota(jnp.int32, (XH, 128), 1)
    edge = (lane < 2) | (lane >= 126)
    tiles = [fixes[pl.ds(LOW, XH), pl.ds(t * 128, 128)] for t in range(2)]

    copies[0].wait()
    for y in range(YH):
        line = y + LOW
        turned = pltpu.roll(tiles[line // 32], (254 - 4 * (line % 32)) % 128, 1)
        if y < CY:
            own = hart[pl.ds(y, CX, stride=CY), :]
        else:
            own = hart_above[pl.ds(y - CY, CX, stride=16), :]
        source = jnp.concatenate([own, hart_right[pl.ds(y * 16, 16), :]], axis=0)
        if 2 <= y < 22:
            bulk = bulk1_ref[pl.ds((y - 2) * XH, XH), :]
        else:
            bulk = bulk2_ref[pl.ds((y if y < 2 else y - 20) * XH, XH), :]
        field[pl.ds(y * XH, XH), :] = (source + bulk) + jnp.where(edge, turned, 0.0)

    step_z = lax.broadcasted_iota(jnp.int32, (16, 128), 1)
    group = step_z // 16
    step_z = step_z % 16
    count = plan_ref[65]
    first_x, first_y = lax.axis_index("dx") * CX, lax.axis_index("dyz") * CY
    first_z = band * CZ

    def window(atom):
        rx, ry, rz = root_ref[0, atom] - first_x, root_ref[1, atom] - first_y, root_ref[2, atom] - first_z
        shift = 128 - (rz & 127)
        inside = ((step_z + rz) & 511) < 128
        halves = []
        for jh in range(2):
            value = jnp.zeros((16, 128), F32)
            for jl in range(8):
                rows = field[pl.ds((ry + (jh * 8 + jl)) * XH + rx, 16), :]
                turned = pltpu.roll(rows, (shift + jl * 16) & 127, 1)
                value = jnp.where(group == jl, turned, value)
            halves.append(jnp.where(inside, value, 0.0))
        return halves

    def atom_step(i, carry):
        items = [2 * i, jnp.minimum(2 * i + 1, count - 1)]
        atoms = [plan_ref[item] for item in items]
        values = [window(atom) for atom in atoms]
        for atom, halves in zip(atoms, values):
            for jh in range(2):
                windows[pl.ds(atom + jh * 1024, 16, stride=64), :] = halves[jh]
        return carry

    lax.fori_loop(0, (count + 1) // 2, atom_step, 0)

    copies[1].wait()
    pad = jnp.zeros((7, 128), F32)
    total = jnp.zeros((128, 128), F32)
    for i in range(16):
        rows = [windows[pl.ds(jh * 1024 + i * 64, 64), :] for jh in range(2)]
        high, low = split(jnp.concatenate(rows, axis=1))
        both = jnp.concatenate([high, low], axis=0)
        shaped = []
        for c in (2 * i, 2 * i + 1):
            first, second = [cells[pl.ds(2 * c + s, NL, stride=64), :] for s in range(2)]
            shaped.append(jnp.concatenate([first, pad, second, pad], axis=0))
        shaped = jnp.concatenate(split(jnp.concatenate(shaped, axis=1)), axis=0)
        total = total + lax.dot_general(both, shaped, (((1,), (1,)), ((), ())), preferred_element_type=F32)
    total = (total[:64] + total[64:]) * GRID_H**3
    total = total + pltpu.roll(total, 64, 1)
    kind = kinds_ref[0]
    moments = jnp.where(kind == 0, total, 0.0) + jnp.where(kind == 1, pltpu.roll(total, 96, 1), 0.0)
    moments = jnp.where(lax.broadcasted_iota(jnp.int32, (64, 128), 1) < 32, moments, 0.0)
    joined = moments[:16]
    for g in range(1, 4):
        joined = joined + pltpu.roll(moments[g * 16 : g * 16 + 16], 32 * g, 1)
    for b in range(4):
        part_ref[b] = joined


def own_kernel(field_ref, out_ref):
    for y in range(CY):
        out_ref[pl.ds(y, CX, stride=CY), :] = field_ref[pl.ds(y * XH, CX), :]


def apply_kernel(
    parts_ref, coupling_ref, base_ref, kinds_ref, proj_ref, ham_ref, out_ref, spread_ref
):
    kind = kinds_ref[1]
    joined = (parts_ref[0] + parts_ref[1]) + (parts_ref[2] + parts_ref[3])
    rows = [joined] + [pltpu.roll(joined, 128 - 32 * g, 1) for g in range(1, 4)]
    moments = jnp.concatenate(rows, axis=0)
    moments = jnp.where(lax.broadcasted_iota(jnp.int32, (64, 128), 1) < 32, moments, 0.0)
    moments = jnp.where(kind == 0, moments, jnp.where(kind == 1, pltpu.roll(moments, 32, 1), 0.0))
    pad = jnp.zeros((7, 256), F32)
    tensors = jnp.concatenate([coupling_ref[0], pad, coupling_ref[1], pad, jnp.zeros((64, 256), F32)], axis=0)
    ham = jnp.where(kind[:, :1] < 2, dot3(moments, tensors) + base_ref[...], 0.0)
    ham_ref[...] = ham
    lane = lax.broadcasted_iota(jnp.int32, (64, 128), 1)
    row = lax.broadcasted_iota(jnp.int32, (64, 128), 0)
    mine = (lane // 16) == (row % 8)
    halves = [pltpu.roll(ham[:, s : s + 128], 0, 1, stride=16, stride_axis=0) for s in (0, 128)]
    for i in range(16):
        placed = halves[i // 8]
        if i % 8:
            placed = pltpu.roll(placed, 128 - (i % 8) * 16, 1)
        spread_ref[pl.ds(i, 64, stride=16), :] = jnp.where(mine, placed, 0.0)
    for g in range(8):
        rows = pl.ds(g * 128, 128)
        out_ref[rows, :] = dot3(spread_ref[rows, :], proj_ref[rows, :])


def far(value):
    return pltpu.with_memory_space_constraint(value, pltpu.HBM)


def close(value):
    return pltpu.with_memory_space_constraint(value, pltpu.VMEM)


def vmem(count):
    return [pl.BlockSpec(memory_space=pltpu.VMEM)] * count


def anywhere(count):
    return [pl.BlockSpec(memory_space=pl.ANY)] * count


def hbm(count):
    return [pl.BlockSpec(memory_space=pltpu.HBM)] * count


def smem(count):
    return [pl.BlockSpec(memory_space=pltpu.SMEM)] * count


def call(kernel, name, outs, specs, scratch=()):
    return pl.pallas_call(
        kernel,
        out_shape=outs,
        in_specs=specs,
        out_specs=tuple(vmem(len(outs))),
        scratch_shapes=list(scratch),
        compiler_params=PARAMS,
        name=name,
    )


def shape(*dims, dtype=F32):
    return jax.ShapeDtypeStruct(dims, dtype)


def local(
    density, hartree, box_root, species, atom_count, shape_functions, coupling, coulomb, rho_ij, projections
):
    slots = box_root.shape[1]

    dens_low, dens_high, hart_low = call(
        lift_kernel,
        "lift",
        (shape(DUP, CY, CZ), shape(LOW, CY, CZ), shape(CX, 16, CZ)),
        hbm(2),
        [pltpu.SemaphoreType.DMA((3,))],
    )(far(density), far(hartree))
    below = shifted(dens_high, "dx", 1)
    above = shifted(dens_low, "dx", -1)
    hart_above = shifted(hart_low, "dyz", -1)

    plan, kinds = pl.pallas_call(
        plan_kernel,
        out_shape=(shape(66, dtype=jnp.int32), shape(2, 64, 128)),
        in_specs=smem(2) + hbm(2),
        out_specs=(smem(1)[0], vmem(1)[0]),
        scratch_shapes=[
            pltpu.VMEM((3, 64), jnp.int32),
            pltpu.VMEM((1, 64), jnp.int32),
            pltpu.SemaphoreType.DMA((2,)),
        ],
        compiler_params=PARAMS,
        name="plan",
    )(box_root, atom_count, far(box_root), far(species.reshape(1, slots)))
    wide_d, send_down, send_up = call(
        widen_kernel,
        "widen",
        (shape(CY * XD, CZ), shape(DUP * XD, CZ), shape(LOW * XD, CZ)),
        anywhere(1) + vmem(3),
    )(close(kinds), density, above, below)
    from_up = shifted(send_down, "dyz", -1)
    from_down = shifted(send_up, "dyz", 1)

    bulk1, tail, own_ends = call(
        inner_kernel,
        "inner",
        (shape(20 * XH, CZ), shape(10 * XD, CZ), shape(XD, 256)),
        vmem(1),
        [pltpu.VMEM((22 * XD, CZ), F32), pltpu.VMEM((22 * XD, CZ), F32)],
    )(wide_d)
    send_right = call(turn_kernel, "turn", (shape(40 * 16, CZ),), anywhere(2) + vmem(2))(
        close(from_down), close(own_ends), hartree, hart_above
    )[0]
    hart_right = shifted(send_right, "dx", -1)

    ends, send_ends = call(ends_kernel, "ends", (shape(XD, 256), pltpu.VMEM((4, XD, 128), F32)), vmem(3))(
        close(own_ends), close(from_up), close(from_down)
    )

    beside = lax.all_to_all(send_ends, "band", 0, 0)
    cells = shape_functions.transpose(1, 0, 2).reshape(NL, 2, 32, 128).transpose(0, 2, 1, 3).reshape(NL * 64, 128)
    bulk2, wrap = call(
        outer_kernel,
        "outer",
        (shape(19 * XH, CZ), shape(4, XD, 256)),
        vmem(4),
        [pltpu.VMEM((n * XD, CZ), F32) for n in (4, 3, 4, 19, 19, 19)],
    )(close(from_up), close(from_down), close(tail), close(ends))

    field, parts = call(
        field_kernel,
        "field",
        (pltpu.VMEM((YH * XH, CZ), F32), pltpu.VMEM((4, 16, 128), F32)),
        smem(2) + hbm(2) + vmem(8),
        [
            pltpu.VMEM((CX * CY, CZ), F32),
            pltpu.VMEM((NL * 64, 128), F32),
            pltpu.VMEM((2 * 16 * 64, 128), F32),
            pltpu.VMEM((XD, 256), F32),
            pltpu.SemaphoreType.DMA((2,)),
        ],
    )(
        box_root, plan,
        far(hartree.reshape(CX * CY, CZ)), far(cells),
        close(hart_above.reshape(CX * 16, CZ)), close(hart_right), close(bulk1), close(bulk2), close(ends), close(beside), close(wrap), close(kinds),
    )

    summed = lax.all_to_all(parts, "band", 0, 0)
    potential = call(own_kernel, "own", (shape(CX * CY, CZ),), vmem(1))(field)[0]
    base = call(base_kernel, "base", (shape(64, 256),), anywhere(1) + vmem(3))(
        parts, rho_ij, coulomb, kinds
    )[0]
    atom_hamiltonian, applied = call(
        apply_kernel,
        "apply",
        (shape(64, 256), shape(64 * NI, 128)),
        vmem(5),
        [pltpu.VMEM((64 * NI, 128), F32)],
    )(summed, coupling, base, kinds, projections.reshape(slots * NI, CZ))
    return (
        potential.reshape(CX, CY, CZ),
        atom_hamiltonian,
        applied.reshape(slots, NI, CZ),
    )


def solution(mesh):
    in_specs = (
        P("dx", "dyz", "band"),
        P("dx", "dyz", "band"),
        P(None, ("dx", "dyz")),
        P(("dx", "dyz")),
        P(("dx", "dyz")),
        P(),
        P(),
        P(),
        P(("dx", "dyz"), None),
        P(("dx", "dyz"), None, "band"),
    )
    out_specs = (P("dx", "dyz", "band"), P(("dx", "dyz"), None), P(("dx", "dyz"), None, "band"))
    return jax.shard_map(local, mesh=mesh, in_specs=in_specs, out_specs=out_specs, check_vma=False)
```

```python
import math

import jax
import jax.numpy as jnp
from jax import lax
from jax.experimental import pallas as pl
from jax.experimental.pallas import tpu as pltpu
from jax.sharding import PartitionSpec as P

BOX = 16
NI = 16
NL = 25
GRID_H = 0.15
HALF = 0.5 / GRID_H
KAPPA = 0.804
MU = 0.2195149727645171
A0 = -0.75 * (3.0 / math.pi) ** (1.0 / 3.0)
C0 = 4.0 * (3.0 * math.pi**2) ** (2.0 / 3.0)

CX, CY, CZ = 32, 24, 128
LOW = 2
DUP = 17
HUP = 15
XD = 56
XH = 48
YD = CY + LOW + DUP
YH = CY + HUP
F32, BF16 = jnp.float32, jnp.bfloat16
PARAMS = pltpu.CompilerParams(vmem_limit_bytes=16 * 1024 * 1024)


def shifted(block, axis, distance):
    n = lax.axis_size(axis)
    return lax.ppermute(block, axis, [(i, (i + distance) % n) for i in range(n)])


def split(value):
    high = value.astype(BF16)
    low = (value - high.astype(F32)).astype(BF16)
    return high, low


def dot(left, right):
    return jnp.dot(left, right, preferred_element_type=F32)


def dot3(left, right):
    lh, ll = split(left)
    rh, rl = split(right)
    return dot(lh, rh) + (dot(ll, rh) + dot(lh, rl))


def column(row):
    shape = (64, 64)
    diagonal = lax.broadcasted_iota(jnp.int32, shape, 0) == lax.broadcasted_iota(jnp.int32, shape, 1)
    spread = jnp.broadcast_to(row.astype(F32), shape)
    return jnp.sum(jnp.where(diagonal, spread, 0.0), axis=1, keepdims=True)


def base_kernel(after_ref, rho_ref, coulomb_ref, coupling_ref, kinds_ref, proj_ref, base_ref, tensor_ref, halves_ref):
    rho = rho_ref[...]
    kind = kinds_ref[1, :, :1]
    total = jnp.zeros((64, 256), F32)
    for s in range(2):
        total = total + dot3(jnp.where(kind == s, rho, 0.0), coulomb_ref[s])
    base_ref[...] = 2.0 * total
    pad = jnp.zeros((7, 256), F32)
    rows = [coupling_ref[0], pad, coupling_ref[1], pad, jnp.zeros((64, 256), F32)]
    tensor_ref[0], tensor_ref[1] = split(jnp.concatenate(rows, axis=0))
    halves_ref[0], halves_ref[1] = split(proj_ref[...])


def lift_kernel(dens_ref, hart_ref, low_ref, high_ref, lines_ref, rim_ref, dens, hart, sems):
    copies = [
        pltpu.make_async_copy(dens_ref.at[pl.ds(0, DUP * CY)], low_ref, sems.at[0]),
        pltpu.make_async_copy(dens_ref.at[pl.ds((CX - LOW) * CY, LOW * CY)], high_ref, sems.at[1]),
        pltpu.make_async_copy(dens_ref, dens, sems.at[2]),
        pltpu.make_async_copy(hart_ref, hart, sems.at[3]),
    ]
    for copy in copies:
        copy.start()
    copies[2].wait()
    for y in range(DUP):
        lines_ref[y * CX : (y + 1) * CX] = dens[pl.ds(y, CX, stride=CY), :]
    copies[3].wait()
    for y in range(HUP):
        lines_ref[(DUP + y) * CX : (DUP + y + 1) * CX] = hart[pl.ds(y, CX, stride=CY), :]
    for x in range(16):
        rim_ref[pl.ds(x, CY, stride=16), :] = hart[x * CY : (x + 1) * CY]
    for copy in copies[:2]:
        copy.wait()


def widen_kernel(dens_ref, above_ref, below_ref, ed_ref, side_ref, up_ref):
    def plane(ref, x):
        return ref[pl.ds(x * CY, CY), :]

    ones = jnp.ones((CY, CZ), F32)
    halo = {-2: plane(below_ref, 0), -1: plane(below_ref, 1)}
    for x in range(DUP):
        halo[CX + x] = plane(above_ref, x)
    for s in range(XD):
        x = s - LOW
        ed_ref[pl.ds(s, CY, stride=XD), :] = plane(dens_ref, x) if 0 <= x < CX else halo.get(x, ones)
    for k in range(24):
        value = halo[CX + k] if k < DUP else halo.get(k - DUP - LOW, ones)
        side_ref[pl.ds(k, DUP, stride=24), :] = value[:DUP]
    up_ref[...] = ed_ref[(CY - LOW) * XD :]


def corner_kernel(after_ref, rim_ref, corner_ref):
    corner_ref[...] = rim_ref[: HUP * 16]


def packed(own, tile, lines, group):
    for line, rows in lines:
        if line // 32 == tile:
            turned = pltpu.roll(rows, (4 * (line % 32) + 2) % 128, 1)
            own = jnp.where(group == line % 32, turned, own)
    return own


def line_group():
    return lax.broadcasted_iota(jnp.int32, (XD, 128), 1) // 4


def ends_kernel(own_ref, lines_ref, side_ref, up_ref, ends_ref, out_ref, down_ref, send_ref, sem):
    group = line_group()
    for i in range(DUP):
        base, side = i * XD, i * 24
        down_ref[base : base + LOW] = side_ref[side + DUP : side + DUP + LOW]
        down_ref[base + LOW : base + LOW + CX] = lines_ref[i * CX : (i + 1) * CX]
        down_ref[base + LOW + CX : base + LOW + CX + DUP] = side_ref[side : side + DUP]
        down_ref[base + LOW + CX + DUP : base + XD] = jnp.ones((XD - LOW - CX - DUP, CZ), F32)
    lines = [(0, up_ref[:XD]), (1, up_ref[XD:])]
    lines += [(LOW + CY + i, down_ref[i * XD : (i + 1) * XD]) for i in range(DUP)]
    tiles = [packed(own_ref[:, pl.ds(t * 128, 128)], t, lines, group) for t in range(2)]
    place = lax.broadcasted_iota(jnp.int32, (XD, 128), 1) % 4
    to_below = jnp.where(place >= 2, tiles[0], pltpu.roll(tiles[1], 126, 1))
    to_above = jnp.where(place < 2, tiles[0], pltpu.roll(tiles[1], 2, 1))
    below = (lax.axis_index("band") + 3) & 3
    for b in range(4):
        send_ref[b] = jnp.where(below == b, to_below, to_above)
    copy = pltpu.make_async_copy(send_ref, out_ref, sem)
    copy.start()
    for t in range(2):
        ends_ref[:, pl.ds(t * 128, 128)] = tiles[t]
    copy.wait()


def slopes(dens, sigma):
    power = jnp.log2(dens)
    root = jnp.exp2(power * (1.0 / 3.0))
    inv = jnp.exp2(power * (-4.0 / 3.0))
    scaled = sigma * (inv * inv)
    below = 1.0 + (MU / (KAPPA * C0)) * scaled
    t = pl.reciprocal(below, approx=True)
    t = t * (2.0 - below * t)
    tt = t * t
    slope_s = (A0 * MU / C0) * (inv * tt)
    slope_n = root * (
        (A0 * 4.0 / 3.0 * (1.0 + KAPPA) - (A0 * 4.0 / 3.0 * KAPPA) * t)
        - (A0 * 8.0 / 3.0 * MU / C0) * (scaled * tt)
    )
    return slope_n, slope_s


def line_flux(center, x_up, x_down, y_up, y_down):
    gx = (x_up - x_down) * HALF
    gy = (y_up - y_down) * HALF
    gz = (pltpu.roll(center, 127, 1) - pltpu.roll(center, 1, 1)) * HALF
    slope_n, slope_s = slopes(center, gx * gx + gy * gy + gz * gz)
    fx, fy, fz = slope_s * gx, slope_s * gy, slope_s * gz
    spread = (pltpu.roll(fx, XD - 1, 0) - pltpu.roll(fx, 1, 0)) + (
        pltpu.roll(fz, 127, 1) - pltpu.roll(fz, 1, 1)
    )
    return slope_n - (2.0 * HALF) * spread, fy


def flux_lines(source, first, count, local_ref, flux_ref, target):
    def step(i, carry):
        base = pl.multiple_of((first + i) * XD, 8)
        goal = pl.ds(pl.multiple_of((target + i) * XD, 8), XD)
        part, flux = line_flux(
            source[pl.ds(base, XD), :],
            source[pl.ds(base + 1, XD), :],
            source[pl.ds(base - 1, XD), :],
            source[pl.ds(pl.multiple_of(base + XD, 8), XD), :],
            source[pl.ds(pl.multiple_of(base - XD, 8), XD), :],
        )
        local_ref[goal, :] = part
        flux_ref[goal, :] = flux
        return carry

    lax.fori_loop(0, count, step, 0, unroll=2)


def packed_flux(dens):
    gx = (pltpu.roll(dens, XD - 1, 0) - pltpu.roll(dens, 1, 0)) * HALF
    gy = (pltpu.roll(dens, 252, 1) - pltpu.roll(dens, 4, 1)) * HALF
    gz = (pltpu.roll(dens, 255, 1) - pltpu.roll(dens, 1, 1)) * HALF
    slope_n, slope_s = slopes(dens, gx * gx + gy * gy + gz * gz)
    return slope_n, slope_s * gx, slope_s * gy, slope_s * gz


def bulk_lines(part, flux, first, count, bulk_ref):
    def step(i, carry):
        base = (first + i) * XD + LOW
        spread = flux[pl.ds(base + XD, XH), :] - flux[pl.ds(base - XD, XH), :]
        goal = pl.ds(pl.multiple_of(i * XH, 8), XH)
        bulk_ref[goal, :] = part[pl.ds(base, XH), :] - (2.0 * HALF) * spread
        return carry

    lax.fori_loop(0, count, step, 0, unroll=2)


def inner_kernel(ed_ref, bulk_ref, tail_ref, ends_ref, part, flux):
    group = line_group()
    lines = [(LOW + i, ed_ref[i * XD : (i + 1) * XD]) for i in range(CY)]
    for tile in range(2):
        ends_ref[:, pl.ds(tile * 128, 128)] = packed(jnp.ones((XD, 128), F32), tile, lines, group)
    flux_lines(ed_ref, 1, 22, part, flux, 0)
    bulk_lines(part, flux, 1, 20, bulk_ref)
    tail_ref[: 2 * XD] = flux[: 2 * XD]
    tail_ref[2 * XD : 4 * XD] = flux[20 * XD :]
    tail_ref[4 * XD : 5 * XD] = part[:XD]
    tail_ref[5 * XD : 6 * XD] = part[21 * XD :]
    tail_ref[6 * XD : 8 * XD] = ed_ref[: 2 * XD]
    tail_ref[8 * XD :] = ed_ref[22 * XD :]


def list_atoms(root_ref, rows_ref, species_ref, count, plan_ref, kinds_ref):
    first_x, first_y = lax.axis_index("dx") * CX, lax.axis_index("dyz") * CY
    first_z = lax.axis_index("band") * CZ

    def step(i, found):
        for atom in [4 * i + k for k in range(4)]:
            offset = (root_ref[2, atom] - first_z) & 511
            meets = (atom < count) & ((offset < CZ) | (offset > 512 - BOX))
            x, y = root_ref[0, atom] - first_x, root_ref[1, atom] - first_y
            plan_ref[found] = x | (y << 5) | (offset << 10) | (atom << 19)
            found = found + meets.astype(jnp.int32)
        return found

    plan_ref[65] = lax.fori_loop(0, (count + 3) // 4, step, 0)
    offset = (rows_ref[2:3, :] - first_z) & 511
    live = lax.broadcasted_iota(jnp.int32, (1, 64), 1) < count
    meets = live & ((offset < CZ) | (offset > 512 - BOX))
    for i, here in enumerate((meets, live)):
        kinds_ref[i] = jnp.broadcast_to(column(jnp.where(here, species_ref[...], 2)), (64, 128))


def outer_kernel(
    count_ref, down_ref, up_ref, tail_ref, ends_ref, root_hbm, species_hbm,
    bulk_ref, wrap_ref, plan_ref, kinds_ref,
    near, near_part, near_flux, far, part, flux, roots, root_rows, species, sems,
):
    copies = [
        pltpu.make_async_copy(root_hbm, roots, sems.at[0]),
        pltpu.make_async_copy(root_hbm, root_rows, sems.at[1]),
        pltpu.make_async_copy(species_hbm, species, sems.at[2]),
    ]
    for copy in copies:
        copy.start()
    near[: 2 * XD] = up_ref[...]
    near[2 * XD :] = tail_ref[6 * XD : 8 * XD]
    near_flux[2 * XD :] = tail_ref[: 2 * XD]
    near_part[2 * XD :] = tail_ref[4 * XD : 5 * XD]
    far[: 2 * XD] = tail_ref[8 * XD :]
    far[2 * XD :] = down_ref[...]
    flux[: 2 * XD] = tail_ref[2 * XD : 4 * XD]
    part[XD : 2 * XD] = tail_ref[5 * XD : 6 * XD]
    flux_lines(near, 1, 2, near_part, near_flux, 0)
    flux_lines(far, 1, DUP, part, flux, 2)
    bulk_lines(near_part, near_flux, 1, 2, bulk_ref.at[pl.ds(0, 2 * XH)])
    bulk_lines(part, flux, 1, DUP, bulk_ref.at[pl.ds(2 * XH, DUP * XH)])
    for i, value in enumerate(packed_flux(ends_ref[...])):
        wrap_ref[i] = value
    for copy in copies:
        copy.wait()
    list_atoms(roots, root_rows, species, count_ref[0], plan_ref, kinds_ref)


def field_kernel(
    plan_ref,
    hart_ref, cells_ref,
    rim_ref, lines_ref, corner_ref, bulk1_ref, bulk2_ref, ends_ref, beside_ref, wrap_ref, kinds_ref,
    field, part_ref,
    hart, cells, windows, fixes, sems,
):
    copies = [
        pltpu.make_async_copy(hart_ref, hart, sems.at[0]),
        pltpu.make_async_copy(cells_ref, cells, sems.at[1]),
    ]
    for copy in copies:
        copy.start()
    place = lax.broadcasted_iota(jnp.int32, (XD, 256), 1) % 4
    middle = (place == 1) | (place == 2)
    low = place < 2
    own = ends_ref[...]

    def fix(dens):
        dn, dx, dy, dz = [
            jnp.where(middle, value - wrap_ref[i], 0.0) for i, value in enumerate(packed_flux(dens))
        ]
        spread = (
            (pltpu.roll(dx, XD - 1, 0) - pltpu.roll(dx, 1, 0))
            + (pltpu.roll(dy, 252, 1) - pltpu.roll(dy, 4, 1))
            + (pltpu.roll(dz, 255, 1) - pltpu.roll(dz, 1, 1))
        )
        return dn - (2.0 * HALF) * spread

    band = lax.axis_index("band")
    after = beside_ref[(band + 1) & 3]
    before = beside_ref[(band + 3) & 3]
    after = jnp.concatenate([after, pltpu.roll(after, 2, 1)], axis=1)
    before = jnp.concatenate([before, pltpu.roll(before, 126, 1)], axis=1)
    top = fix(jnp.where(low, own, after))
    bottom = fix(jnp.where(low, before, own))
    fixes[...] = jnp.where(low, top, bottom)

    lane = lax.broadcasted_iota(jnp.int32, (XH, 128), 1)
    edge = (lane < 2) | (lane >= 126)
    tiles = [fixes[pl.ds(LOW, XH), pl.ds(t * 128, 128)] for t in range(2)]

    copies[0].wait()
    for y in range(YH):
        line = y + LOW
        turned = pltpu.roll(tiles[line // 32], (254 - 4 * (line % 32)) % 128, 1)
        if y < CY:
            own = hart[pl.ds(y, CX, stride=CY), :]
            rim = rim_ref[pl.ds(y * 16, 16), :]
        else:
            own = lines_ref[pl.ds((DUP + y - CY) * CX, CX), :]
            rim = corner_ref[pl.ds((y - CY) * 16, 16), :]
        source = jnp.concatenate([own, rim], axis=0)
        if 2 <= y < 22:
            bulk = bulk1_ref[pl.ds((y - 2) * XH, XH), :]
        else:
            bulk = bulk2_ref[pl.ds((y if y < 2 else y - 20) * XH, XH), :]
        field[pl.ds(y * XH, XH), :] = (source + bulk) + jnp.where(edge, turned, 0.0)

    step_z = lax.broadcasted_iota(jnp.int32, (16, 128), 1)
    group = step_z // 16
    step_z = step_z % 16
    count = plan_ref[65]

    def window(entry):
        rx, ry, rz = entry & 31, (entry >> 5) & 31, (entry >> 10) & 511
        shift = 128 - (rz & 127)
        inside = ((step_z + rz) & 511) < 128
        halves = []
        for jh in range(2):
            value = jnp.zeros((16, 128), F32)
            for jl in range(8):
                rows = field[pl.ds((ry + (jh * 8 + jl)) * XH + rx, 16), :]
                turned = pltpu.roll(rows, (shift + jl * 16) & 127, 1)
                value = jnp.where(group == jl, turned, value)
            halves.append(jnp.where(inside, value, 0.0))
        return halves

    def atom_step(i, carry):
        items = [2 * i, jnp.minimum(2 * i + 1, count - 1)]
        entries = [plan_ref[item] for item in items]
        values = [window(entry) for entry in entries]
        atoms = [entry >> 19 for entry in entries]
        for atom, halves in zip(atoms, values):
            for jh in range(2):
                windows[pl.ds(atom + jh * 1024, 16, stride=64), :] = halves[jh]
        return carry

    lax.fori_loop(0, (count + 1) // 2, atom_step, 0)

    copies[1].wait()
    pad = jnp.zeros((7, 128), F32)
    total = jnp.zeros((128, 128), F32)
    for i in range(16):
        rows = [windows[pl.ds(jh * 1024 + i * 64, 64), :] for jh in range(2)]
        high, low = split(jnp.concatenate(rows, axis=1))
        both = jnp.concatenate([high, low], axis=0)
        shaped = []
        for c in (2 * i, 2 * i + 1):
            first, second = [cells[pl.ds(2 * c + s, NL, stride=64), :] for s in range(2)]
            shaped.append(jnp.concatenate([first, pad, second, pad], axis=0))
        shaped = jnp.concatenate(split(jnp.concatenate(shaped, axis=1)), axis=0)
        total = total + lax.dot_general(both, shaped, (((1,), (1,)), ((), ())), preferred_element_type=F32)
    total = (total[:64] + total[64:]) * GRID_H**3
    total = total + pltpu.roll(total, 64, 1)
    kind = kinds_ref[0]
    moments = jnp.where(kind == 0, total, 0.0) + jnp.where(kind == 1, pltpu.roll(total, 96, 1), 0.0)
    moments = jnp.where(lax.broadcasted_iota(jnp.int32, (64, 128), 1) < 32, moments, 0.0)
    joined = moments[:16]
    for g in range(1, 4):
        joined = joined + pltpu.roll(moments[g * 16 : g * 16 + 16], 32 * g, 1)
    for b in range(4):
        part_ref[b] = joined


def own_kernel(field_ref, out_ref):
    for y in range(CY):
        out_ref[pl.ds(y, CX, stride=CY), :] = field_ref[pl.ds(y * XH, CX), :]


def apply_kernel(
    parts_ref, tensor_ref, base_ref, kinds_ref, halves_ref, ham_out, out_ref, spread_ref, ham_ref, rows_ref, sems
):
    kind = kinds_ref[1]
    joined = (parts_ref[0] + parts_ref[1]) + (parts_ref[2] + parts_ref[3])
    rows = [joined] + [pltpu.roll(joined, 128 - 32 * g, 1) for g in range(1, 4)]
    moments = jnp.concatenate(rows, axis=0)
    moments = jnp.where(lax.broadcasted_iota(jnp.int32, (64, 128), 1) < 32, moments, 0.0)
    moments = jnp.where(kind == 0, moments, jnp.where(kind == 1, pltpu.roll(moments, 32, 1), 0.0))
    high, low = split(moments)
    ham = dot(high, tensor_ref[0]) + (dot(low, tensor_ref[0]) + dot(high, tensor_ref[1]))
    ham = jnp.where(kind[:, :1] < 2, ham + base_ref[...], 0.0)
    ham_ref[...] = ham
    copies = [pltpu.make_async_copy(ham_ref, ham_out, sems.at[4])]
    copies[0].start()
    lane = lax.broadcasted_iota(jnp.int32, (64, 128), 1)
    row = lax.broadcasted_iota(jnp.int32, (64, 128), 0)
    mine = (lane // 16) == (row % 8)
    halves = [pltpu.roll(ham[:, s : s + 128], 0, 1, stride=16, stride_axis=0) for s in (0, 128)]
    for i in range(16):
        placed = halves[i // 8]
        if i % 8:
            placed = pltpu.roll(placed, 128 - (i % 8) * 16, 1)
        spread_ref[pl.ds(i, 64, stride=16), :] = jnp.where(mine, placed, 0.0)
    for g in range(8):
        rows = pl.ds(g * 128, 128)
        high, low = split(spread_ref[rows, :])
        first = halves_ref[0, rows, :]
        rows_ref[rows, :] = dot(high, first) + (dot(low, first) + dot(high, halves_ref[1, rows, :]))
        if g % 2:
            part = pl.ds((g - 1) * 128, 256)
            copies.append(pltpu.make_async_copy(rows_ref.at[part], out_ref.at[part], sems.at[g // 2]))
            copies[-1].start()
    for copy in copies:
        copy.wait()


def far(value):
    return pltpu.with_memory_space_constraint(value, pltpu.HBM)


def close(value):
    return pltpu.with_memory_space_constraint(value, pltpu.VMEM)


def vmem(count):
    return [pl.BlockSpec(memory_space=pltpu.VMEM)] * count


def anywhere(count):
    return [pl.BlockSpec(memory_space=pl.ANY)] * count


def hbm(count):
    return [pl.BlockSpec(memory_space=pltpu.HBM)] * count


def smem(count):
    return [pl.BlockSpec(memory_space=pltpu.SMEM)] * count


def call(kernel, name, outs, specs, scratch=()):
    return pl.pallas_call(
        kernel,
        out_shape=outs,
        in_specs=specs,
        out_specs=tuple(vmem(len(outs))),
        scratch_shapes=list(scratch),
        compiler_params=PARAMS,
        name=name,
    )


def shape(*dims, dtype=F32):
    return jax.ShapeDtypeStruct(dims, dtype)


def local(
    density, hartree, box_root, species, atom_count, shape_functions, coupling, coulomb, rho_ij, projections
):
    slots = box_root.shape[1]

    dens_rows, hart_rows = density.reshape(CX * CY, CZ), hartree.reshape(CX * CY, CZ)
    low, high, lines, rim = call(
        lift_kernel,
        "lift",
        (shape(DUP * CY, CZ), shape(LOW * CY, CZ), shape((DUP + HUP) * CX, CZ), shape(CY * 16, CZ)),
        hbm(2),
        [pltpu.VMEM((CX * CY, CZ), F32), pltpu.VMEM((CX * CY, CZ), F32), pltpu.SemaphoreType.DMA((4,))],
    )(far(dens_rows), far(hart_rows))
    above = shifted(low, "dx", -1)
    below = shifted(high, "dx", 1)
    rim = shifted(rim, "dx", -1)
    lines_above = shifted(lines, "dyz", -1)

    wide_d, side, send_up = call(
        widen_kernel,
        "widen",
        (shape(CY * XD, CZ), shape(DUP * 24, CZ), shape(LOW * XD, CZ)),
        vmem(3),
    )(dens_rows, above, below)
    side_above = shifted(side, "dyz", -1)
    from_down = shifted(send_up, "dyz", 1)

    bulk1, tail, own_ends = call(
        inner_kernel,
        "inner",
        (shape(20 * XH, CZ), shape(10 * XD, CZ), shape(XD, 256)),
        vmem(1),
        [pltpu.VMEM((22 * XD, CZ), F32), pltpu.VMEM((22 * XD, CZ), F32)],
    )(wide_d)

    corner = call(corner_kernel, "corner", (shape(HUP * 16, CZ),), anywhere(1) + vmem(1))(
        close(own_ends), close(rim)
    )[0]
    corner = shifted(corner, "dyz", -1)

    ends, send_ends, from_up = pl.pallas_call(
        ends_kernel,
        out_shape=(shape(XD, 256), pltpu.HBM((4, XD, 128), F32), shape(DUP * XD, CZ)),
        in_specs=vmem(4),
        out_specs=tuple(vmem(1) + hbm(1) + vmem(1)),
        scratch_shapes=[pltpu.VMEM((4, XD, 128), F32), pltpu.SemaphoreType.DMA(())],
        compiler_params=PARAMS,
        name="ends",
    )(close(own_ends), close(lines_above), close(side_above), close(from_down))

    beside = lax.all_to_all(send_ends, "band", 0, 0)
    cells = shape_functions.transpose(1, 0, 2).reshape(NL, 2, 32, 128).transpose(0, 2, 1, 3).reshape(NL * 64, 128)
    bulk2, wrap, plan, kinds = pl.pallas_call(
        outer_kernel,
        out_shape=(
            shape(19 * XH, CZ),
            shape(4, XD, 256),
            shape(66, dtype=jnp.int32),
            shape(2, 64, 128),
        ),
        in_specs=smem(1) + vmem(4) + hbm(2),
        out_specs=tuple(vmem(2) + smem(1) + vmem(1)),
        scratch_shapes=[pltpu.VMEM((n * XD, CZ), F32) for n in (4, 3, 4, 19, 19, 19)]
        + [
            pltpu.SMEM((3, 64), jnp.int32),
            pltpu.VMEM((3, 64), jnp.int32),
            pltpu.VMEM((1, 64), jnp.int32),
            pltpu.SemaphoreType.DMA((3,)),
        ],
        compiler_params=PARAMS,
        name="outer",
    )(
        atom_count,
        close(from_up), close(from_down), close(tail), close(ends),
        far(box_root), far(species.reshape(1, slots)),
    )

    field, parts = call(
        field_kernel,
        "field",
        (pltpu.VMEM((YH * XH, CZ), F32), pltpu.VMEM((4, 16, 128), F32)),
        smem(1) + hbm(2) + vmem(9),
        [
            pltpu.VMEM((CX * CY, CZ), F32),
            pltpu.VMEM((NL * 64, 128), F32),
            pltpu.VMEM((2 * 16 * 64, 128), F32),
            pltpu.VMEM((XD, 256), F32),
            pltpu.SemaphoreType.DMA((2,)),
        ],
    )(
        plan,
        far(hart_rows), far(cells),
        close(rim), close(lines_above), close(corner), close(bulk1), close(bulk2), close(ends), close(beside), close(wrap), close(kinds),
    )

    summed = lax.all_to_all(parts, "band", 0, 0)
    potential = call(own_kernel, "own", (shape(CX * CY, CZ),), vmem(1))(field)[0]
    base, tensors, halves = call(
        base_kernel,
        "base",
        (shape(64, 256), shape(2, 128, 256, dtype=BF16), shape(2, 64 * NI, 128, dtype=BF16)),
        anywhere(1) + vmem(5),
    )(parts, rho_ij, coulomb, coupling, close(kinds), projections.reshape(slots * NI, CZ))
    atom_hamiltonian, applied = pl.pallas_call(
        apply_kernel,
        out_shape=(pltpu.HBM((64, 256), F32), pltpu.HBM((64 * NI, 128), F32)),
        in_specs=vmem(5),
        out_specs=tuple(hbm(2)),
        scratch_shapes=[
            pltpu.VMEM((64 * NI, 128), F32),
            pltpu.VMEM((64, 256), F32),
            pltpu.VMEM((64 * NI, 128), F32),
            pltpu.SemaphoreType.DMA((5,)),
        ],
        compiler_params=PARAMS,
        name="apply",
    )(close(summed), close(tensors), close(base), close(kinds), close(halves))
    return (
        potential.reshape(CX, CY, CZ),
        atom_hamiltonian,
        applied.reshape(slots, NI, CZ),
    )


def solution(mesh):
    in_specs = (
        P("dx", "dyz", "band"),
        P("dx", "dyz", "band"),
        P(None, ("dx", "dyz")),
        P(("dx", "dyz")),
        P(("dx", "dyz")),
        P(),
        P(),
        P(),
        P(("dx", "dyz"), None),
        P(("dx", "dyz"), None, "band"),
    )
    out_specs = (P("dx", "dyz", "band"), P(("dx", "dyz"), None), P(("dx", "dyz"), None, "band"))
    return jax.shard_map(local, mesh=mesh, in_specs=in_specs, out_specs=out_specs, check_vma=False)
```

```python
import math

import jax
import jax.numpy as jnp
from jax import lax
from jax.experimental import pallas as pl
from jax.experimental.pallas import tpu as pltpu
from jax.sharding import PartitionSpec as P

BOX = 16
NI = 16
NL = 25
GRID_H = 0.15
HALF = 0.5 / GRID_H
KAPPA = 0.804
MU = 0.2195149727645171
A0 = -0.75 * (3.0 / math.pi) ** (1.0 / 3.0)
C0 = 4.0 * (3.0 * math.pi**2) ** (2.0 / 3.0)

CX, CY, CZ = 32, 24, 128
LOW = 2
DUP = 17
HUP = 15
XD = 56
XH = 48
YD = CY + LOW + DUP
YH = CY + HUP
F32, BF16 = jnp.float32, jnp.bfloat16
PARAMS = pltpu.CompilerParams(vmem_limit_bytes=16 * 1024 * 1024)


def shifted(block, axis, distance):
    n = lax.axis_size(axis)
    return lax.ppermute(block, axis, [(i, (i + distance) % n) for i in range(n)])


def split(value):
    high = value.astype(BF16)
    low = (value - high.astype(F32)).astype(BF16)
    return high, low


def dot(left, right):
    return jnp.dot(left, right, preferred_element_type=F32)


def dot3(left, right):
    lh, ll = split(left)
    rh, rl = split(right)
    return dot(lh, rh) + (dot(ll, rh) + dot(lh, rl))


def column(row):
    shape = (64, 64)
    diagonal = lax.broadcasted_iota(jnp.int32, shape, 0) == lax.broadcasted_iota(jnp.int32, shape, 1)
    spread = jnp.broadcast_to(row.astype(F32), shape)
    return jnp.sum(jnp.where(diagonal, spread, 0.0), axis=1, keepdims=True)


def base_kernel(after_ref, rho_ref, coulomb_ref, coupling_ref, kinds_ref, proj_ref, base_ref, tensor_ref, halves_ref):
    rho = rho_ref[...]
    kind = kinds_ref[1, :, :1]
    total = jnp.zeros((64, 256), F32)
    for s in range(2):
        total = total + dot3(jnp.where(kind == s, rho, 0.0), coulomb_ref[s])
    base_ref[...] = 2.0 * total
    pad = jnp.zeros((7, 256), F32)
    rows = [coupling_ref[0], pad, coupling_ref[1], pad, jnp.zeros((64, 256), F32)]
    tensor_ref[0], tensor_ref[1] = split(jnp.concatenate(rows, axis=0))
    halves_ref[0], halves_ref[1] = split(proj_ref[...])


def lift_kernel(dens_ref, hart_ref, low_ref, high_ref, lines_ref, rim_ref, dens, hart, sems):
    copies = [
        pltpu.make_async_copy(dens_ref.at[pl.ds(0, DUP * CY)], low_ref, sems.at[0]),
        pltpu.make_async_copy(dens_ref.at[pl.ds((CX - LOW) * CY, LOW * CY)], high_ref, sems.at[1]),
        pltpu.make_async_copy(dens_ref, dens, sems.at[2]),
        pltpu.make_async_copy(hart_ref, hart, sems.at[3]),
    ]
    for copy in copies:
        copy.start()
    copies[2].wait()
    for y in range(DUP):
        lines_ref[y * CX : (y + 1) * CX] = dens[pl.ds(y, CX, stride=CY), :]
    copies[3].wait()
    for y in range(HUP):
        lines_ref[(DUP + y) * CX : (DUP + y + 1) * CX] = hart[pl.ds(y, CX, stride=CY), :]
    for x in range(16):
        rim_ref[pl.ds(x, CY, stride=16), :] = hart[x * CY : (x + 1) * CY]
    for copy in copies[:2]:
        copy.wait()


def widen_kernel(dens_ref, above_ref, below_ref, ed_ref, side_ref, up_ref):
    def plane(ref, x):
        return ref[pl.ds(x * CY, CY), :]

    ones = jnp.ones((CY, CZ), F32)
    halo = {-2: plane(below_ref, 0), -1: plane(below_ref, 1)}
    for x in range(DUP):
        halo[CX + x] = plane(above_ref, x)
    for s in range(XD):
        x = s - LOW
        ed_ref[pl.ds(s, CY, stride=XD), :] = plane(dens_ref, x) if 0 <= x < CX else halo.get(x, ones)
    for k in range(24):
        value = halo[CX + k] if k < DUP else halo.get(k - DUP - LOW, ones)
        side_ref[pl.ds(k, DUP, stride=24), :] = value[:DUP]
    up_ref[...] = ed_ref[(CY - LOW) * XD :]


def corner_kernel(after_ref, rim_ref, corner_ref):
    corner_ref[...] = rim_ref[: HUP * 16]


def packed(own, tile, lines, group):
    for line, rows in lines:
        if line // 32 == tile:
            turned = pltpu.roll(rows, (4 * (line % 32) + 2) % 128, 1)
            own = jnp.where(group == line % 32, turned, own)
    return own


def line_group():
    return lax.broadcasted_iota(jnp.int32, (XD, 128), 1) // 4


def join_lines(target, first, lines_ref, side_ref):
    for i in range(DUP):
        base, side = first + i * XD, i * 24
        target[base : base + LOW] = side_ref[side + DUP : side + DUP + LOW]
        target[base + LOW : base + LOW + CX] = lines_ref[i * CX : (i + 1) * CX]
        target[base + LOW + CX : base + LOW + CX + DUP] = side_ref[side : side + DUP]
        target[base + LOW + CX + DUP : base + XD] = jnp.ones((XD - LOW - CX - DUP, CZ), F32)


def ends_kernel(own_ref, lines_ref, side_ref, up_ref, ends_ref, out_ref, down_ref, send_ref, sem):
    group = line_group()
    join_lines(down_ref, 0, lines_ref, side_ref)
    lines = [(0, up_ref[:XD]), (1, up_ref[XD:])]
    lines += [(LOW + CY + i, down_ref[i * XD : (i + 1) * XD]) for i in range(DUP)]
    tiles = [packed(own_ref[:, pl.ds(t * 128, 128)], t, lines, group) for t in range(2)]
    place = lax.broadcasted_iota(jnp.int32, (XD, 128), 1) % 4
    to_below = jnp.where(place >= 2, tiles[0], pltpu.roll(tiles[1], 126, 1))
    to_above = jnp.where(place < 2, tiles[0], pltpu.roll(tiles[1], 2, 1))
    below = (lax.axis_index("band") + 3) & 3
    for b in range(4):
        send_ref[b] = jnp.where(below == b, to_below, to_above)
    copy = pltpu.make_async_copy(send_ref, out_ref, sem)
    copy.start()
    for t in range(2):
        ends_ref[:, pl.ds(t * 128, 128)] = tiles[t]
    copy.wait()


def slopes(dens, sigma):
    power = jnp.log2(dens)
    root = jnp.exp2(power * (1.0 / 3.0))
    inv = jnp.exp2(power * (-4.0 / 3.0))
    scaled = sigma * (inv * inv)
    below = 1.0 + (MU / (KAPPA * C0)) * scaled
    t = pl.reciprocal(below, approx=True)
    t = t * (2.0 - below * t)
    tt = t * t
    slope_s = (A0 * MU / C0) * (inv * tt)
    slope_n = root * (
        (A0 * 4.0 / 3.0 * (1.0 + KAPPA) - (A0 * 4.0 / 3.0 * KAPPA) * t)
        - (A0 * 8.0 / 3.0 * MU / C0) * (scaled * tt)
    )
    return slope_n, slope_s


def line_flux(center, x_up, x_down, y_up, y_down):
    gx = (x_up - x_down) * HALF
    gy = (y_up - y_down) * HALF
    gz = (pltpu.roll(center, 127, 1) - pltpu.roll(center, 1, 1)) * HALF
    slope_n, slope_s = slopes(center, gx * gx + gy * gy + gz * gz)
    fx, fy, fz = slope_s * gx, slope_s * gy, slope_s * gz
    spread = (pltpu.roll(fx, XD - 1, 0) - pltpu.roll(fx, 1, 0)) + (
        pltpu.roll(fz, 127, 1) - pltpu.roll(fz, 1, 1)
    )
    return slope_n - (2.0 * HALF) * spread, fy


def flux_lines(source, first, count, local_ref, flux_ref, target):
    def step(i, carry):
        base = pl.multiple_of((first + i) * XD, 8)
        goal = pl.ds(pl.multiple_of((target + i) * XD, 8), XD)
        part, flux = line_flux(
            source[pl.ds(base, XD), :],
            source[pl.ds(base + 1, XD), :],
            source[pl.ds(base - 1, XD), :],
            source[pl.ds(pl.multiple_of(base + XD, 8), XD), :],
            source[pl.ds(pl.multiple_of(base - XD, 8), XD), :],
        )
        local_ref[goal, :] = part
        flux_ref[goal, :] = flux
        return carry

    lax.fori_loop(0, count, step, 0, unroll=2)


def packed_flux(dens):
    gx = (pltpu.roll(dens, XD - 1, 0) - pltpu.roll(dens, 1, 0)) * HALF
    gy = (pltpu.roll(dens, 252, 1) - pltpu.roll(dens, 4, 1)) * HALF
    gz = (pltpu.roll(dens, 255, 1) - pltpu.roll(dens, 1, 1)) * HALF
    slope_n, slope_s = slopes(dens, gx * gx + gy * gy + gz * gz)
    return slope_n, slope_s * gx, slope_s * gy, slope_s * gz


def bulk_lines(part, flux, first, count, bulk_ref):
    def step(i, carry):
        base = (first + i) * XD + LOW
        spread = flux[pl.ds(base + XD, XH), :] - flux[pl.ds(base - XD, XH), :]
        goal = pl.ds(pl.multiple_of(i * XH, 8), XH)
        bulk_ref[goal, :] = part[pl.ds(base, XH), :] - (2.0 * HALF) * spread
        return carry

    lax.fori_loop(0, count, step, 0, unroll=2)


def inner_kernel(ed_ref, hart_hbm, bulk_ref, tail_ref, ends_ref, part, flux, hart, sem):
    copy = pltpu.make_async_copy(hart_hbm, hart, sem)
    copy.start()
    group = line_group()
    lines = [(LOW + i, ed_ref[i * XD : (i + 1) * XD]) for i in range(CY)]
    for tile in range(2):
        ends_ref[:, pl.ds(tile * 128, 128)] = packed(jnp.ones((XD, 128), F32), tile, lines, group)
    flux_lines(ed_ref, 1, 22, part, flux, 0)
    bulk_lines(part, flux, 1, 20, bulk_ref)
    copy.wait()
    for i in range(20):
        here = slice(i * XH, i * XH + CX)
        bulk_ref[here] = bulk_ref[here] + hart[pl.ds(i + 2, CX, stride=CY), :]
    tail_ref[: 2 * XD] = flux[: 2 * XD]
    tail_ref[2 * XD : 4 * XD] = flux[20 * XD :]
    tail_ref[4 * XD : 5 * XD] = part[:XD]
    tail_ref[5 * XD : 6 * XD] = part[21 * XD :]
    tail_ref[6 * XD : 8 * XD] = ed_ref[: 2 * XD]
    tail_ref[8 * XD :] = ed_ref[22 * XD :]


def list_atoms(root_ref, rows_ref, species_ref, count, plan_ref, kinds_ref):
    first_x, first_y = lax.axis_index("dx") * CX, lax.axis_index("dyz") * CY
    first_z = lax.axis_index("band") * CZ

    def step(i, found):
        for atom in [4 * i + k for k in range(4)]:
            offset = (root_ref[2, atom] - first_z) & 511
            meets = (atom < count) & ((offset < CZ) | (offset > 512 - BOX))
            x, y = root_ref[0, atom] - first_x, root_ref[1, atom] - first_y
            plan_ref[found] = x | (y << 5) | (offset << 10) | (atom << 19)
            found = found + meets.astype(jnp.int32)
        return found

    plan_ref[65] = lax.fori_loop(0, (count + 3) // 4, step, 0)
    offset = (rows_ref[2:3, :] - first_z) & 511
    live = lax.broadcasted_iota(jnp.int32, (1, 64), 1) < count
    meets = live & ((offset < CZ) | (offset > 512 - BOX))
    for i, here in enumerate((meets, live)):
        kinds_ref[i] = jnp.broadcast_to(column(jnp.where(here, species_ref[...], 2)), (64, 128))


def outer_kernel(
    count_ref, side_ref, up_ref, tail_ref, ends_ref, lines_ref, root_hbm, species_hbm, hart_hbm,
    bulk_ref, wrap_ref, plan_ref, kinds_ref,
    near, near_part, near_flux, far, part, flux, roots, root_rows, species, hart, sems,
):
    copies = [
        pltpu.make_async_copy(root_hbm, roots, sems.at[0]),
        pltpu.make_async_copy(root_hbm, root_rows, sems.at[1]),
        pltpu.make_async_copy(species_hbm, species, sems.at[2]),
        pltpu.make_async_copy(hart_hbm, hart, sems.at[3]),
    ]
    for copy in copies:
        copy.start()
    near[: 2 * XD] = up_ref[...]
    near[2 * XD :] = tail_ref[6 * XD : 8 * XD]
    near_flux[2 * XD :] = tail_ref[: 2 * XD]
    near_part[2 * XD :] = tail_ref[4 * XD : 5 * XD]
    far[: 2 * XD] = tail_ref[8 * XD :]
    join_lines(far, 2 * XD, lines_ref, side_ref)
    flux[: 2 * XD] = tail_ref[2 * XD : 4 * XD]
    part[XD : 2 * XD] = tail_ref[5 * XD : 6 * XD]
    flux_lines(near, 1, 2, near_part, near_flux, 0)
    flux_lines(far, 1, DUP, part, flux, 2)
    bulk_lines(near_part, near_flux, 1, 2, bulk_ref.at[pl.ds(0, 2 * XH)])
    bulk_lines(part, flux, 1, DUP, bulk_ref.at[pl.ds(2 * XH, DUP * XH)])
    for i, value in enumerate(packed_flux(ends_ref[...])):
        wrap_ref[i] = value
    for copy in copies:
        copy.wait()
    for i in range(2 + DUP):
        y = i if i < 2 else i + 20
        here = slice(i * XH, i * XH + CX)
        if y < CY:
            own = hart[pl.ds(y, CX, stride=CY), :]
        else:
            own = lines_ref[(DUP + y - CY) * CX : (DUP + y - CY + 1) * CX]
        bulk_ref[here] = bulk_ref[here] + own
    list_atoms(roots, root_rows, species, count_ref[0], plan_ref, kinds_ref)


def field_kernel(
    plan_ref,
    cells_ref,
    rim_ref, corner_ref, bulk1_ref, bulk2_ref, ends_ref, beside_ref, wrap_ref, kinds_ref,
    field, part_ref,
    cells, windows, fixes, sem,
):
    copy = pltpu.make_async_copy(cells_ref, cells, sem)
    copy.start()
    place = lax.broadcasted_iota(jnp.int32, (XD, 256), 1) % 4
    middle = (place == 1) | (place == 2)
    low = place < 2
    own = ends_ref[...]

    def fix(dens):
        dn, dx, dy, dz = [
            jnp.where(middle, value - wrap_ref[i], 0.0) for i, value in enumerate(packed_flux(dens))
        ]
        spread = (
            (pltpu.roll(dx, XD - 1, 0) - pltpu.roll(dx, 1, 0))
            + (pltpu.roll(dy, 252, 1) - pltpu.roll(dy, 4, 1))
            + (pltpu.roll(dz, 255, 1) - pltpu.roll(dz, 1, 1))
        )
        return dn - (2.0 * HALF) * spread

    band = lax.axis_index("band")
    after = beside_ref[(band + 1) & 3]
    before = beside_ref[(band + 3) & 3]
    after = jnp.concatenate([after, pltpu.roll(after, 2, 1)], axis=1)
    before = jnp.concatenate([before, pltpu.roll(before, 126, 1)], axis=1)
    top = fix(jnp.where(low, own, after))
    bottom = fix(jnp.where(low, before, own))
    fixes[...] = jnp.where(low, top, bottom)

    lane = lax.broadcasted_iota(jnp.int32, (XH, 128), 1)
    edge = (lane < 2) | (lane >= 126)
    tiles = [fixes[pl.ds(LOW, XH), pl.ds(t * 128, 128)] for t in range(2)]

    for y in range(YH):
        line = y + LOW
        turned = pltpu.roll(tiles[line // 32], (254 - 4 * (line % 32)) % 128, 1)
        if 2 <= y < 22:
            bulk = bulk1_ref[pl.ds((y - 2) * XH, XH), :]
        else:
            bulk = bulk2_ref[pl.ds((y if y < 2 else y - 20) * XH, XH), :]
        value = bulk + jnp.where(edge, turned, 0.0)
        if y < CY:
            rim = rim_ref[pl.ds(y * 16, 16), :]
        else:
            rim = corner_ref[pl.ds((y - CY) * 16, 16), :]
        field[pl.ds(y * XH, CX), :] = value[:CX]
        field[pl.ds(y * XH + CX, 16), :] = value[CX:] + rim

    step_z = lax.broadcasted_iota(jnp.int32, (16, 128), 1)
    group = step_z // 16
    step_z = step_z % 16
    count = plan_ref[65]

    def window(entry):
        rx, ry, rz = entry & 31, (entry >> 5) & 31, (entry >> 10) & 511
        shift = 128 - (rz & 127)
        inside = ((step_z + rz) & 511) < 128
        halves = []
        for jh in range(2):
            value = jnp.zeros((16, 128), F32)
            for jl in range(8):
                rows = field[pl.ds((ry + (jh * 8 + jl)) * XH + rx, 16), :]
                turned = pltpu.roll(rows, (shift + jl * 16) & 127, 1)
                value = jnp.where(group == jl, turned, value)
            halves.append(jnp.where(inside, value, 0.0))
        return halves

    def atom_step(i, carry):
        items = [4 * i] + [jnp.minimum(4 * i + k, count - 1) for k in range(1, 4)]
        entries = [plan_ref[item] for item in items]
        values = [window(entry) for entry in entries]
        atoms = [entry >> 19 for entry in entries]
        for atom, halves in zip(atoms, values):
            for jh in range(2):
                windows[pl.ds(atom + jh * 1024, 16, stride=64), :] = halves[jh]
        return carry

    lax.fori_loop(0, (count + 3) // 4, atom_step, 0)

    copy.wait()
    pad = jnp.zeros((7, 128), F32)
    total = jnp.zeros((128, 128), F32)
    for i in range(16):
        rows = [windows[pl.ds(jh * 1024 + i * 64, 64), :] for jh in range(2)]
        high, low = split(jnp.concatenate(rows, axis=1))
        both = jnp.concatenate([high, low], axis=0)
        shaped = []
        for c in (2 * i, 2 * i + 1):
            first, second = [cells[pl.ds(2 * c + s, NL, stride=64), :] for s in range(2)]
            shaped.append(jnp.concatenate([first, pad, second, pad], axis=0))
        shaped = jnp.concatenate(split(jnp.concatenate(shaped, axis=1)), axis=0)
        total = total + lax.dot_general(both, shaped, (((1,), (1,)), ((), ())), preferred_element_type=F32)
    total = (total[:64] + total[64:]) * GRID_H**3
    total = total + pltpu.roll(total, 64, 1)
    kind = kinds_ref[0]
    moments = jnp.where(kind == 0, total, 0.0) + jnp.where(kind == 1, pltpu.roll(total, 96, 1), 0.0)
    moments = jnp.where(lax.broadcasted_iota(jnp.int32, (64, 128), 1) < 32, moments, 0.0)
    joined = moments[:16]
    for g in range(1, 4):
        joined = joined + pltpu.roll(moments[g * 16 : g * 16 + 16], 32 * g, 1)
    for b in range(4):
        part_ref[b] = joined


def own_kernel(field_ref, out_ref):
    for y in range(CY):
        out_ref[pl.ds(y, CX, stride=CY), :] = field_ref[pl.ds(y * XH, CX), :]


def apply_kernel(
    parts_ref, tensor_ref, base_ref, kinds_ref, halves_ref, ham_out, out_ref, spread_ref, ham_ref, rows_ref, sems
):
    kind = kinds_ref[1]
    joined = (parts_ref[0] + parts_ref[1]) + (parts_ref[2] + parts_ref[3])
    rows = [joined] + [pltpu.roll(joined, 128 - 32 * g, 1) for g in range(1, 4)]
    moments = jnp.concatenate(rows, axis=0)
    moments = jnp.where(lax.broadcasted_iota(jnp.int32, (64, 128), 1) < 32, moments, 0.0)
    moments = jnp.where(kind == 0, moments, jnp.where(kind == 1, pltpu.roll(moments, 32, 1), 0.0))
    high, low = split(moments)
    ham = dot(high, tensor_ref[0]) + (dot(low, tensor_ref[0]) + dot(high, tensor_ref[1]))
    ham = jnp.where(kind[:, :1] < 2, ham + base_ref[...], 0.0)
    ham_ref[...] = ham
    copies = [pltpu.make_async_copy(ham_ref, ham_out, sems.at[4])]
    copies[0].start()
    lane = lax.broadcasted_iota(jnp.int32, (64, 128), 1)
    row = lax.broadcasted_iota(jnp.int32, (64, 128), 0)
    mine = (lane // 16) == (row % 8)
    halves = [pltpu.roll(ham[:, s : s + 128], 0, 1, stride=16, stride_axis=0) for s in (0, 128)]
    for i in range(16):
        placed = halves[i // 8]
        if i % 8:
            placed = pltpu.roll(placed, 128 - (i % 8) * 16, 1)
        spread_ref[pl.ds(i, 64, stride=16), :] = jnp.where(mine, placed, 0.0)
    for g in range(8):
        rows = pl.ds(g * 128, 128)
        high, low = split(spread_ref[rows, :])
        first = halves_ref[0, rows, :]
        rows_ref[rows, :] = dot(high, first) + (dot(low, first) + dot(high, halves_ref[1, rows, :]))
        if g % 2:
            part = pl.ds((g - 1) * 128, 256)
            copies.append(pltpu.make_async_copy(rows_ref.at[part], out_ref.at[part], sems.at[g // 2]))
            copies[-1].start()
    for copy in copies:
        copy.wait()


def far(value):
    return pltpu.with_memory_space_constraint(value, pltpu.HBM)


def close(value):
    return pltpu.with_memory_space_constraint(value, pltpu.VMEM)


def vmem(count):
    return [pl.BlockSpec(memory_space=pltpu.VMEM)] * count


def anywhere(count):
    return [pl.BlockSpec(memory_space=pl.ANY)] * count


def hbm(count):
    return [pl.BlockSpec(memory_space=pltpu.HBM)] * count


def smem(count):
    return [pl.BlockSpec(memory_space=pltpu.SMEM)] * count


def call(kernel, name, outs, specs, scratch=()):
    return pl.pallas_call(
        kernel,
        out_shape=outs,
        in_specs=specs,
        out_specs=tuple(vmem(len(outs))),
        scratch_shapes=list(scratch),
        compiler_params=PARAMS,
        name=name,
    )


def shape(*dims, dtype=F32):
    return jax.ShapeDtypeStruct(dims, dtype)


def local(
    density, hartree, box_root, species, atom_count, shape_functions, coupling, coulomb, rho_ij, projections
):
    slots = box_root.shape[1]

    dens_rows, hart_rows = density.reshape(CX * CY, CZ), hartree.reshape(CX * CY, CZ)
    low, high, lines, rim = call(
        lift_kernel,
        "lift",
        (shape(DUP * CY, CZ), shape(LOW * CY, CZ), shape((DUP + HUP) * CX, CZ), shape(CY * 16, CZ)),
        hbm(2),
        [pltpu.VMEM((CX * CY, CZ), F32), pltpu.VMEM((CX * CY, CZ), F32), pltpu.SemaphoreType.DMA((4,))],
    )(far(dens_rows), far(hart_rows))
    above = shifted(low, "dx", -1)
    below = shifted(high, "dx", 1)
    rim = shifted(rim, "dx", -1)
    lines_above = shifted(lines, "dyz", -1)

    wide_d, side, send_up = call(
        widen_kernel,
        "widen",
        (shape(CY * XD, CZ), shape(DUP * 24, CZ), shape(LOW * XD, CZ)),
        vmem(3),
    )(dens_rows, above, below)
    side_above = shifted(side, "dyz", -1)
    from_down = shifted(send_up, "dyz", 1)

    bulk1, tail, own_ends = call(
        inner_kernel,
        "inner",
        (shape(20 * XH, CZ), shape(10 * XD, CZ), shape(XD, 256)),
        vmem(1) + hbm(1),
        [
            pltpu.VMEM((22 * XD, CZ), F32),
            pltpu.VMEM((22 * XD, CZ), F32),
            pltpu.VMEM((CX * CY, CZ), F32),
            pltpu.SemaphoreType.DMA(()),
        ],
    )(wide_d, far(hart_rows))

    corner = call(corner_kernel, "corner", (shape(HUP * 16, CZ),), anywhere(1) + vmem(1))(
        close(own_ends), close(rim)
    )[0]
    corner = shifted(corner, "dyz", -1)

    ends, send_ends = pl.pallas_call(
        ends_kernel,
        out_shape=(shape(XD, 256), pltpu.HBM((4, XD, 128), F32)),
        in_specs=vmem(4),
        out_specs=tuple(vmem(1) + hbm(1)),
        scratch_shapes=[pltpu.VMEM((DUP * XD, CZ), F32), pltpu.VMEM((4, XD, 128), F32), pltpu.SemaphoreType.DMA(())],
        compiler_params=PARAMS,
        name="ends",
    )(close(own_ends), close(lines_above), close(side_above), close(from_down))

    beside = lax.all_to_all(send_ends, "band", 0, 0)
    cells = shape_functions.transpose(1, 0, 2).reshape(NL, 2, 32, 128).transpose(0, 2, 1, 3).reshape(NL * 64, 128)
    bulk2, wrap, plan, kinds = pl.pallas_call(
        outer_kernel,
        out_shape=(
            shape(19 * XH, CZ),
            shape(4, XD, 256),
            shape(66, dtype=jnp.int32),
            shape(2, 64, 128),
        ),
        in_specs=smem(1) + vmem(5) + hbm(3),
        out_specs=tuple(vmem(2) + smem(1) + vmem(1)),
        scratch_shapes=[pltpu.VMEM((n * XD, CZ), F32) for n in (4, 3, 4, 19, 19, 19)]
        + [
            pltpu.SMEM((3, 64), jnp.int32),
            pltpu.VMEM((3, 64), jnp.int32),
            pltpu.VMEM((1, 64), jnp.int32),
            pltpu.VMEM((CX * CY, CZ), F32),
            pltpu.SemaphoreType.DMA((4,)),
        ],
        compiler_params=PARAMS,
        name="outer",
    )(
        atom_count,
        close(side_above), close(from_down), close(tail), close(ends), close(lines_above),
        far(box_root), far(species.reshape(1, slots)), far(hart_rows),
    )

    field, parts = call(
        field_kernel,
        "field",
        (pltpu.VMEM((YH * XH, CZ), F32), pltpu.VMEM((4, 16, 128), F32)),
        smem(1) + hbm(1) + vmem(8),
        [
            pltpu.VMEM((NL * 64, 128), F32),
            pltpu.VMEM((2 * 16 * 64, 128), F32),
            pltpu.VMEM((XD, 256), F32),
            pltpu.SemaphoreType.DMA(()),
        ],
    )(
        plan,
        far(cells),
        close(rim), close(corner), close(bulk1), close(bulk2), close(ends), close(beside), close(wrap), close(kinds),
    )

    summed = lax.all_to_all(parts, "band", 0, 0)
    potential = call(own_kernel, "own", (shape(CX * CY, CZ),), vmem(1))(field)[0]
    base, tensors, halves = call(
        base_kernel,
        "base",
        (shape(64, 256), shape(2, 128, 256, dtype=BF16), shape(2, 64 * NI, 128, dtype=BF16)),
        anywhere(1) + vmem(5),
    )(parts, rho_ij, coulomb, coupling, close(kinds), projections.reshape(slots * NI, CZ))
    atom_hamiltonian, applied = pl.pallas_call(
        apply_kernel,
        out_shape=(pltpu.HBM((64, 256), F32), pltpu.HBM((64 * NI, 128), F32)),
        in_specs=vmem(5),
        out_specs=tuple(hbm(2)),
        scratch_shapes=[
            pltpu.VMEM((64 * NI, 128), F32),
            pltpu.VMEM((64, 256), F32),
            pltpu.VMEM((64 * NI, 128), F32),
            pltpu.SemaphoreType.DMA((5,)),
        ],
        compiler_params=PARAMS,
        name="apply",
    )(close(summed), close(tensors), close(base), close(kinds), close(halves))
    return (
        potential.reshape(CX, CY, CZ),
        atom_hamiltonian,
        applied.reshape(slots, NI, CZ),
    )


def solution(mesh):
    in_specs = (
        P("dx", "dyz", "band"),
        P("dx", "dyz", "band"),
        P(None, ("dx", "dyz")),
        P(("dx", "dyz")),
        P(("dx", "dyz")),
        P(),
        P(),
        P(),
        P(("dx", "dyz"), None),
        P(("dx", "dyz"), None, "band"),
    )
    out_specs = (P("dx", "dyz", "band"), P(("dx", "dyz"), None), P(("dx", "dyz"), None, "band"))
    return jax.shard_map(local, mesh=mesh, in_specs=in_specs, out_specs=out_specs, check_vma=False)
```

```python
import math

import jax
import jax.numpy as jnp
from jax import lax
from jax.experimental import pallas as pl
from jax.experimental.pallas import tpu as pltpu
from jax.sharding import PartitionSpec as P

BOX = 16
NI = 16
NL = 25
GRID_H = 0.15
HALF = 0.5 / GRID_H
KAPPA = 0.804
MU = 0.2195149727645171
A0 = -0.75 * (3.0 / math.pi) ** (1.0 / 3.0)
C0 = 4.0 * (3.0 * math.pi**2) ** (2.0 / 3.0)

CX, CY, CZ = 32, 24, 128
LOW = 2
DUP = 17
HUP = 15
XD = 56
XH = 48
YD = CY + LOW + DUP
YH = CY + HUP
F32, BF16 = jnp.float32, jnp.bfloat16
PARAMS = pltpu.CompilerParams(vmem_limit_bytes=16 * 1024 * 1024)


def shifted(block, axis, distance):
    n = lax.axis_size(axis)
    return lax.ppermute(block, axis, [(i, (i + distance) % n) for i in range(n)])


def split(value):
    high = value.astype(BF16)
    low = (value - high.astype(F32)).astype(BF16)
    return high, low


def dot(left, right):
    return jnp.dot(left, right, preferred_element_type=F32)


def dot3(left, right):
    lh, ll = split(left)
    rh, rl = split(right)
    return dot(lh, rh) + (dot(ll, rh) + dot(lh, rl))


def column(row):
    shape = (64, 64)
    diagonal = lax.broadcasted_iota(jnp.int32, shape, 0) == lax.broadcasted_iota(jnp.int32, shape, 1)
    spread = jnp.broadcast_to(row.astype(F32), shape)
    return jnp.sum(jnp.where(diagonal, spread, 0.0), axis=1, keepdims=True)


def base_kernel(after_ref, rho_ref, coulomb_ref, coupling_ref, kinds_ref, proj_ref, base_ref, tensor_ref, halves_ref):
    rho = rho_ref[...]
    kind = kinds_ref[1, :, :1]
    total = jnp.zeros((64, 256), F32)
    for s in range(2):
        total = total + dot3(jnp.where(kind == s, rho, 0.0), coulomb_ref[s])
    base_ref[...] = 2.0 * total
    pad = jnp.zeros((7, 256), F32)
    rows = [coupling_ref[0], pad, coupling_ref[1], pad, jnp.zeros((64, 256), F32)]
    tensor_ref[0], tensor_ref[1] = split(jnp.concatenate(rows, axis=0))
    halves_ref[0], halves_ref[1] = split(proj_ref[...])


def lift_kernel(dens_ref, hart_ref, low_ref, high_ref, lines_ref, rim_ref, dens, hart, sems):
    copies = [
        pltpu.make_async_copy(dens_ref.at[pl.ds(0, DUP * CY)], low_ref, sems.at[0]),
        pltpu.make_async_copy(dens_ref.at[pl.ds((CX - LOW) * CY, LOW * CY)], high_ref, sems.at[1]),
        pltpu.make_async_copy(dens_ref, dens, sems.at[2]),
        pltpu.make_async_copy(hart_ref, hart, sems.at[3]),
    ]
    for copy in copies:
        copy.start()
    copies[2].wait()
    for y in range(DUP):
        lines_ref[y * CX : (y + 1) * CX] = dens[pl.ds(y, CX, stride=CY), :]
    copies[3].wait()
    for y in range(HUP):
        lines_ref[(DUP + y) * CX : (DUP + y + 1) * CX] = hart[pl.ds(y, CX, stride=CY), :]
    for x in range(16):
        rim_ref[pl.ds(x, CY, stride=16), :] = hart[x * CY : (x + 1) * CY]
    for copy in copies[:2]:
        copy.wait()


def widen_kernel(dens_ref, above_ref, below_ref, ed_ref, side_ref, up_ref, sides):
    def plane(ref, x):
        return ref[pl.ds(x * CY, CY), :]

    ones = jnp.ones((CY, CZ), F32)
    halo = {-2: plane(below_ref, 0), -1: plane(below_ref, 1)}
    for x in range(DUP):
        halo[CX + x] = plane(above_ref, x)
    for s in range(XD):
        x = s - LOW
        ed_ref[pl.ds(s, CY, stride=XD), :] = plane(dens_ref, x) if 0 <= x < CX else halo.get(x, ones)
    for k in range(24):
        value = halo[CX + k] if k < DUP else halo.get(k - DUP - LOW, ones)
        sides[pl.ds(k, CY, stride=24), :] = value
    side_ref[...] = sides[: DUP * 24]
    up_ref[...] = ed_ref[(CY - LOW) * XD :]


def corner_kernel(after_ref, rim_ref, corner_ref):
    corner_ref[...] = rim_ref[: HUP * 16]


def packed(own, tile, lines, group):
    for line, rows in lines:
        if line // 32 == tile:
            turned = pltpu.roll(rows, (4 * (line % 32) + 2) % 128, 1)
            own = jnp.where(group == line % 32, turned, own)
    return own


def line_group():
    return lax.broadcasted_iota(jnp.int32, (XD, 128), 1) // 4


def join_lines(target, first, lines_ref, side_ref):
    for i in range(DUP):
        base, side = first + i * XD, i * 24
        target[base : base + LOW] = side_ref[side + DUP : side + DUP + LOW]
        target[base + LOW : base + LOW + CX] = lines_ref[i * CX : (i + 1) * CX]
        target[base + LOW + CX : base + LOW + CX + DUP] = side_ref[side : side + DUP]
        target[base + LOW + CX + DUP : base + XD] = jnp.ones((XD - LOW - CX - DUP, CZ), F32)


def ends_kernel(own_ref, lines_ref, side_ref, up_ref, ends_ref, out_ref, down_ref, send_ref, sem):
    group = line_group()
    join_lines(down_ref, 0, lines_ref, side_ref)
    lines = [(0, up_ref[:XD]), (1, up_ref[XD:])]
    lines += [(LOW + CY + i, down_ref[i * XD : (i + 1) * XD]) for i in range(DUP)]
    tiles = [packed(own_ref[:, pl.ds(t * 128, 128)], t, lines, group) for t in range(2)]
    place = lax.broadcasted_iota(jnp.int32, (XD, 128), 1) % 4
    to_below = jnp.where(place >= 2, tiles[0], pltpu.roll(tiles[1], 126, 1))
    to_above = jnp.where(place < 2, tiles[0], pltpu.roll(tiles[1], 2, 1))
    below = (lax.axis_index("band") + 3) & 3
    for b in range(4):
        send_ref[b] = jnp.where(below == b, to_below, to_above)
    copy = pltpu.make_async_copy(send_ref, out_ref, sem)
    copy.start()
    for t in range(2):
        ends_ref[:, pl.ds(t * 128, 128)] = tiles[t]
    copy.wait()


def slopes(dens, sigma):
    power = jnp.log2(dens)
    root = jnp.exp2(power * (1.0 / 3.0))
    inv = jnp.exp2(power * (-4.0 / 3.0))
    scaled = sigma * (inv * inv)
    below = 1.0 + (MU / (KAPPA * C0)) * scaled
    t = pl.reciprocal(below, approx=True)
    t = t * (2.0 - below * t)
    tt = t * t
    slope_s = (A0 * MU / C0) * (inv * tt)
    slope_n = root * (
        (A0 * 4.0 / 3.0 * (1.0 + KAPPA) - (A0 * 4.0 / 3.0 * KAPPA) * t)
        - (A0 * 8.0 / 3.0 * MU / C0) * (scaled * tt)
    )
    return slope_n, slope_s


def line_flux(center, x_up, x_down, y_up, y_down):
    gx = (x_up - x_down) * HALF
    gy = (y_up - y_down) * HALF
    gz = (pltpu.roll(center, 127, 1) - pltpu.roll(center, 1, 1)) * HALF
    slope_n, slope_s = slopes(center, gx * gx + gy * gy + gz * gz)
    fx, fy, fz = slope_s * gx, slope_s * gy, slope_s * gz
    spread = (pltpu.roll(fx, XD - 1, 0) - pltpu.roll(fx, 1, 0)) + (
        pltpu.roll(fz, 127, 1) - pltpu.roll(fz, 1, 1)
    )
    return slope_n - (2.0 * HALF) * spread, fy


def flux_lines(source, first, count, local_ref, flux_ref, target):
    def step(i, carry):
        base = pl.multiple_of((first + i) * XD, 8)
        goal = pl.ds(pl.multiple_of((target + i) * XD, 8), XD)
        part, flux = line_flux(
            source[pl.ds(base, XD), :],
            source[pl.ds(base + 1, XD), :],
            source[pl.ds(base - 1, XD), :],
            source[pl.ds(pl.multiple_of(base + XD, 8), XD), :],
            source[pl.ds(pl.multiple_of(base - XD, 8), XD), :],
        )
        local_ref[goal, :] = part
        flux_ref[goal, :] = flux
        return carry

    lax.fori_loop(0, count, step, 0, unroll=2)


def packed_flux(dens):
    gx = (pltpu.roll(dens, XD - 1, 0) - pltpu.roll(dens, 1, 0)) * HALF
    gy = (pltpu.roll(dens, 252, 1) - pltpu.roll(dens, 4, 1)) * HALF
    gz = (pltpu.roll(dens, 255, 1) - pltpu.roll(dens, 1, 1)) * HALF
    slope_n, slope_s = slopes(dens, gx * gx + gy * gy + gz * gz)
    return slope_n, slope_s * gx, slope_s * gy, slope_s * gz


def bulk_lines(part, flux, first, count, bulk_ref):
    def step(i, carry):
        base = (first + i) * XD + LOW
        spread = flux[pl.ds(base + XD, XH), :] - flux[pl.ds(base - XD, XH), :]
        goal = pl.ds(pl.multiple_of(i * XH, 8), XH)
        bulk_ref[goal, :] = part[pl.ds(base, XH), :] - (2.0 * HALF) * spread
        return carry

    lax.fori_loop(0, count, step, 0, unroll=2)


def inner_kernel(ed_ref, hart_hbm, bulk_ref, tail_ref, ends_ref, part, flux, hart, sem):
    copy = pltpu.make_async_copy(hart_hbm, hart, sem)
    copy.start()
    group = line_group()
    lines = [(LOW + i, ed_ref[i * XD : (i + 1) * XD]) for i in range(CY)]
    for tile in range(2):
        ends_ref[:, pl.ds(tile * 128, 128)] = packed(jnp.ones((XD, 128), F32), tile, lines, group)
    flux_lines(ed_ref, 1, 22, part, flux, 0)
    bulk_lines(part, flux, 1, 20, bulk_ref)
    copy.wait()
    for i in range(20):
        here = slice(i * XH, i * XH + CX)
        bulk_ref[here] = bulk_ref[here] + hart[pl.ds(i + 2, CX, stride=CY), :]
    tail_ref[: 2 * XD] = flux[: 2 * XD]
    tail_ref[2 * XD : 4 * XD] = flux[20 * XD :]
    tail_ref[4 * XD : 5 * XD] = part[:XD]
    tail_ref[5 * XD : 6 * XD] = part[21 * XD :]
    tail_ref[6 * XD : 8 * XD] = ed_ref[: 2 * XD]
    tail_ref[8 * XD :] = ed_ref[22 * XD :]


def list_atoms(root_ref, rows_ref, species_ref, count, plan_ref, kinds_ref):
    first_x, first_y = lax.axis_index("dx") * CX, lax.axis_index("dyz") * CY
    first_z = lax.axis_index("band") * CZ

    def step(i, found):
        for atom in [4 * i + k for k in range(4)]:
            offset = (root_ref[2, atom] - first_z) & 511
            meets = (atom < count) & ((offset < CZ) | (offset > 512 - BOX))
            x, y = root_ref[0, atom] - first_x, root_ref[1, atom] - first_y
            plan_ref[found] = x | (y << 5) | (offset << 10) | (atom << 19)
            found = found + meets.astype(jnp.int32)
        return found

    plan_ref[65] = lax.fori_loop(0, (count + 3) // 4, step, 0)
    offset = (rows_ref[2:3, :] - first_z) & 511
    live = lax.broadcasted_iota(jnp.int32, (1, 64), 1) < count
    meets = live & ((offset < CZ) | (offset > 512 - BOX))
    for i, here in enumerate((meets, live)):
        kinds_ref[i] = jnp.broadcast_to(column(jnp.where(here, species_ref[...], 2)), (64, 128))


def outer_kernel(
    count_ref, side_ref, up_ref, tail_ref, ends_ref, lines_ref, root_hbm, species_hbm, hart_hbm,
    bulk_ref, wrap_ref, plan_ref, kinds_ref,
    near, near_part, near_flux, far, part, flux, roots, root_rows, species, hart, sems,
):
    copies = [
        pltpu.make_async_copy(root_hbm, roots, sems.at[0]),
        pltpu.make_async_copy(root_hbm, root_rows, sems.at[1]),
        pltpu.make_async_copy(species_hbm, species, sems.at[2]),
        pltpu.make_async_copy(hart_hbm, hart, sems.at[3]),
    ]
    for copy in copies:
        copy.start()
    near[: 2 * XD] = up_ref[...]
    near[2 * XD :] = tail_ref[6 * XD : 8 * XD]
    near_flux[2 * XD :] = tail_ref[: 2 * XD]
    near_part[2 * XD :] = tail_ref[4 * XD : 5 * XD]
    far[: 2 * XD] = tail_ref[8 * XD :]
    join_lines(far, 2 * XD, lines_ref, side_ref)
    flux[: 2 * XD] = tail_ref[2 * XD : 4 * XD]
    part[XD : 2 * XD] = tail_ref[5 * XD : 6 * XD]
    flux_lines(near, 1, 2, near_part, near_flux, 0)
    flux_lines(far, 1, DUP, part, flux, 2)
    bulk_lines(near_part, near_flux, 1, 2, bulk_ref.at[pl.ds(0, 2 * XH)])
    bulk_lines(part, flux, 1, DUP, bulk_ref.at[pl.ds(2 * XH, DUP * XH)])
    for i, value in enumerate(packed_flux(ends_ref[...])):
        wrap_ref[i] = value
    for copy in copies:
        copy.wait()
    for i in range(2 + DUP):
        y = i if i < 2 else i + 20
        here = slice(i * XH, i * XH + CX)
        if y < CY:
            own = hart[pl.ds(y, CX, stride=CY), :]
        else:
            own = lines_ref[(DUP + y - CY) * CX : (DUP + y - CY + 1) * CX]
        bulk_ref[here] = bulk_ref[here] + own
    list_atoms(roots, root_rows, species, count_ref[0], plan_ref, kinds_ref)


def field_kernel(
    plan_ref,
    cells_ref,
    rim_ref, corner_ref, bulk1_ref, bulk2_ref, ends_ref, beside_ref, wrap_ref, kinds_ref,
    field, part_ref,
    cells, windows, fixes, sem,
):
    copy = pltpu.make_async_copy(cells_ref, cells.at[pl.ds(0, NL * 64)], sem)
    copy.start()
    place = lax.broadcasted_iota(jnp.int32, (XD, 256), 1) % 4
    middle = (place == 1) | (place == 2)
    low = place < 2
    own = ends_ref[...]

    def fix(dens):
        dn, dx, dy, dz = [
            jnp.where(middle, value - wrap_ref[i], 0.0) for i, value in enumerate(packed_flux(dens))
        ]
        spread = (
            (pltpu.roll(dx, XD - 1, 0) - pltpu.roll(dx, 1, 0))
            + (pltpu.roll(dy, 252, 1) - pltpu.roll(dy, 4, 1))
            + (pltpu.roll(dz, 255, 1) - pltpu.roll(dz, 1, 1))
        )
        return dn - (2.0 * HALF) * spread

    band = lax.axis_index("band")
    after = beside_ref[(band + 1) & 3]
    before = beside_ref[(band + 3) & 3]
    after = jnp.concatenate([after, pltpu.roll(after, 2, 1)], axis=1)
    before = jnp.concatenate([before, pltpu.roll(before, 126, 1)], axis=1)
    top = fix(jnp.where(low, own, after))
    bottom = fix(jnp.where(low, before, own))
    fixes[...] = jnp.where(low, top, bottom)

    lane = lax.broadcasted_iota(jnp.int32, (XH, 128), 1)
    edge = (lane < 2) | (lane >= 126)
    tiles = [fixes[pl.ds(LOW, XH), pl.ds(t * 128, 128)] for t in range(2)]

    for y in range(YH):
        line = y + LOW
        turned = pltpu.roll(tiles[line // 32], (254 - 4 * (line % 32)) % 128, 1)
        if 2 <= y < 22:
            bulk = bulk1_ref[pl.ds((y - 2) * XH, XH), :]
        else:
            bulk = bulk2_ref[pl.ds((y if y < 2 else y - 20) * XH, XH), :]
        value = bulk + jnp.where(edge, turned, 0.0)
        if y < CY:
            rim = rim_ref[pl.ds(y * 16, 16), :]
        else:
            rim = corner_ref[pl.ds((y - CY) * 16, 16), :]
        field[pl.ds(y * XH, CX), :] = value[:CX]
        field[pl.ds(y * XH + CX, 16), :] = value[CX:] + rim

    step_z = lax.broadcasted_iota(jnp.int32, (16, 128), 1)
    group = step_z // 16
    step_z = step_z % 16
    count = plan_ref[65]

    def window(entry):
        rx, ry, rz = entry & 31, (entry >> 5) & 31, (entry >> 10) & 511
        shift = 128 - (rz & 127)
        inside = ((step_z + rz) & 511) < 128
        halves = []
        for jh in range(2):
            value = jnp.zeros((16, 128), F32)
            for jl in range(8):
                rows = field[pl.ds((ry + (jh * 8 + jl)) * XH + rx, 16), :]
                turned = pltpu.roll(rows, (shift + jl * 16) & 127, 1)
                value = jnp.where(group == jl, turned, value)
            halves.append(jnp.where(inside, value, 0.0))
        return halves

    def atom_step(i, carry):
        items = [4 * i] + [jnp.minimum(4 * i + k, count - 1) for k in range(1, 4)]
        entries = [plan_ref[item] for item in items]
        values = [window(entry) for entry in entries]
        atoms = [entry >> 19 for entry in entries]
        for atom, halves in zip(atoms, values):
            for jh in range(2):
                windows[pl.ds(atom + jh * 1024, 16, stride=64), :] = halves[jh]
        return carry

    lax.fori_loop(0, (count + 3) // 4, atom_step, 0)

    copy.wait()
    pad = jnp.zeros((7, 128), F32)
    total = jnp.zeros((128, 128), F32)
    for i in range(16):
        rows = [windows[pl.ds(jh * 1024 + i * 64, 64), :] for jh in range(2)]
        high, low = split(jnp.concatenate(rows, axis=1))
        both = jnp.concatenate([high, low], axis=0)
        shaped = []
        for c in (2 * i, 2 * i + 1):
            first, second = [cells[pl.ds(2 * c + s, NL, stride=64), :] for s in range(2)]
            shaped.append(jnp.concatenate([first, pad, second, pad], axis=0))
        shaped = jnp.concatenate(split(jnp.concatenate(shaped, axis=1)), axis=0)
        total = total + lax.dot_general(both, shaped, (((1,), (1,)), ((), ())), preferred_element_type=F32)
    total = (total[:64] + total[64:]) * GRID_H**3
    total = total + pltpu.roll(total, 64, 1)
    kind = kinds_ref[0]
    moments = jnp.where(kind == 0, total, 0.0) + jnp.where(kind == 1, pltpu.roll(total, 96, 1), 0.0)
    moments = jnp.where(lax.broadcasted_iota(jnp.int32, (64, 128), 1) < 32, moments, 0.0)
    joined = moments[:16]
    for g in range(1, 4):
        joined = joined + pltpu.roll(moments[g * 16 : g * 16 + 16], 32 * g, 1)
    for b in range(4):
        part_ref[b] = joined


def own_kernel(field_ref, out_ref):
    for y in range(CY):
        out_ref[pl.ds(y, CX, stride=CY), :] = field_ref[pl.ds(y * XH, CX), :]


def apply_kernel(
    parts_ref, tensor_ref, base_ref, kinds_ref, halves_ref, ham_out, out_ref, spread_ref, ham_ref, rows_ref, sems
):
    kind = kinds_ref[1]
    joined = (parts_ref[0] + parts_ref[1]) + (parts_ref[2] + parts_ref[3])
    rows = [joined] + [pltpu.roll(joined, 128 - 32 * g, 1) for g in range(1, 4)]
    moments = jnp.concatenate(rows, axis=0)
    moments = jnp.where(lax.broadcasted_iota(jnp.int32, (64, 128), 1) < 32, moments, 0.0)
    moments = jnp.where(kind == 0, moments, jnp.where(kind == 1, pltpu.roll(moments, 32, 1), 0.0))
    high, low = split(moments)
    ham = dot(high, tensor_ref[0]) + (dot(low, tensor_ref[0]) + dot(high, tensor_ref[1]))
    ham = jnp.where(kind[:, :1] < 2, ham + base_ref[...], 0.0)
    ham_ref[...] = ham
    copies = [pltpu.make_async_copy(ham_ref, ham_out, sems.at[4])]
    copies[0].start()
    lane = lax.broadcasted_iota(jnp.int32, (64, 128), 1)
    row = lax.broadcasted_iota(jnp.int32, (64, 128), 0)
    mine = (lane // 16) == (row % 8)
    halves = [pltpu.roll(ham[:, s : s + 128], 0, 1, stride=16, stride_axis=0) for s in (0, 128)]
    for i in range(16):
        placed = halves[i // 8]
        if i % 8:
            placed = pltpu.roll(placed, 128 - (i % 8) * 16, 1)
        spread_ref[pl.ds(i, 64, stride=16), :] = jnp.where(mine, placed, 0.0)
    for g in range(8):
        rows = pl.ds(g * 128, 128)
        high, low = split(spread_ref[rows, :])
        first = halves_ref[0, rows, :]
        rows_ref[rows, :] = dot(high, first) + (dot(low, first) + dot(high, halves_ref[1, rows, :]))
        if g % 2:
            part = pl.ds((g - 1) * 128, 256)
            copies.append(pltpu.make_async_copy(rows_ref.at[part], out_ref.at[part], sems.at[g // 2]))
            copies[-1].start()
    for copy in copies:
        copy.wait()


def far(value):
    return pltpu.with_memory_space_constraint(value, pltpu.HBM)


def close(value):
    return pltpu.with_memory_space_constraint(value, pltpu.VMEM)


def vmem(count):
    return [pl.BlockSpec(memory_space=pltpu.VMEM)] * count


def anywhere(count):
    return [pl.BlockSpec(memory_space=pl.ANY)] * count


def hbm(count):
    return [pl.BlockSpec(memory_space=pltpu.HBM)] * count


def smem(count):
    return [pl.BlockSpec(memory_space=pltpu.SMEM)] * count


def call(kernel, name, outs, specs, scratch=()):
    return pl.pallas_call(
        kernel,
        out_shape=outs,
        in_specs=specs,
        out_specs=tuple(vmem(len(outs))),
        scratch_shapes=list(scratch),
        compiler_params=PARAMS,
        name=name,
    )


def shape(*dims, dtype=F32):
    return jax.ShapeDtypeStruct(dims, dtype)


def local(
    density, hartree, box_root, species, atom_count, shape_functions, coupling, coulomb, rho_ij, projections
):
    slots = box_root.shape[1]

    dens_rows, hart_rows = density.reshape(CX * CY, CZ), hartree.reshape(CX * CY, CZ)
    low, high, lines, rim = call(
        lift_kernel,
        "lift",
        (shape(DUP * CY, CZ), shape(LOW * CY, CZ), shape((DUP + HUP) * CX, CZ), shape(CY * 16, CZ)),
        hbm(2),
        [pltpu.VMEM((CX * CY, CZ), F32), pltpu.VMEM((CX * CY, CZ), F32), pltpu.SemaphoreType.DMA((4,))],
    )(far(dens_rows), far(hart_rows))
    above = shifted(low, "dx", -1)
    below = shifted(high, "dx", 1)
    rim = shifted(rim, "dx", -1)
    lines_above = shifted(lines, "dyz", -1)

    wide_d, side, send_up = call(
        widen_kernel,
        "widen",
        (shape(CY * XD, CZ), shape(DUP * 24, CZ), shape(LOW * XD, CZ)),
        vmem(3),
        [pltpu.VMEM((CY * 24, CZ), F32)],
    )(dens_rows, above, below)
    side_above = shifted(side, "dyz", -1)
    from_down = shifted(send_up, "dyz", 1)

    bulk1, tail, own_ends = call(
        inner_kernel,
        "inner",
        (shape(20 * XH, CZ), shape(10 * XD, CZ), shape(XD, 256)),
        vmem(1) + hbm(1),
        [
            pltpu.VMEM((22 * XD, CZ), F32),
            pltpu.VMEM((22 * XD, CZ), F32),
            pltpu.VMEM((CX * CY, CZ), F32),
            pltpu.SemaphoreType.DMA(()),
        ],
    )(wide_d, far(hart_rows))

    corner = call(corner_kernel, "corner", (shape(HUP * 16, CZ),), anywhere(1) + vmem(1))(
        close(own_ends), close(rim)
    )[0]
    corner = shifted(corner, "dyz", -1)

    ends, send_ends = pl.pallas_call(
        ends_kernel,
        out_shape=(shape(XD, 256), pltpu.HBM((4, XD, 128), F32)),
        in_specs=vmem(4),
        out_specs=tuple(vmem(1) + hbm(1)),
        scratch_shapes=[pltpu.VMEM((DUP * XD + 8, CZ), F32), pltpu.VMEM((4, XD, 128), F32), pltpu.SemaphoreType.DMA(())],
        compiler_params=PARAMS,
        name="ends",
    )(close(own_ends), close(lines_above), close(side_above), close(from_down))

    beside = lax.all_to_all(send_ends, "band", 0, 0)
    cells = shape_functions.transpose(1, 0, 2).reshape(NL, 2, 32, 128).transpose(0, 2, 1, 3).reshape(NL * 64, 128)
    bulk2, wrap, plan, kinds = pl.pallas_call(
        outer_kernel,
        out_shape=(
            shape(19 * XH, CZ),
            shape(4, XD, 256),
            shape(66, dtype=jnp.int32),
            shape(2, 64, 128),
        ),
        in_specs=smem(1) + vmem(5) + hbm(3),
        out_specs=tuple(vmem(2) + smem(1) + vmem(1)),
        scratch_shapes=[pltpu.VMEM((n * XD, CZ), F32) for n in (4, 3, 4, 20, 20, 20)]
        + [
            pltpu.SMEM((3, 64), jnp.int32),
            pltpu.VMEM((3, 64), jnp.int32),
            pltpu.VMEM((1, 64), jnp.int32),
            pltpu.VMEM((CX * CY, CZ), F32),
            pltpu.SemaphoreType.DMA((4,)),
        ],
        compiler_params=PARAMS,
        name="outer",
    )(
        atom_count,
        close(side_above), close(from_down), close(tail), close(ends), close(lines_above),
        far(box_root), far(species.reshape(1, slots)), far(hart_rows),
    )

    field, parts = call(
        field_kernel,
        "field",
        (pltpu.VMEM((YH * XH, CZ), F32), pltpu.VMEM((4, 16, 128), F32)),
        smem(1) + hbm(1) + vmem(8),
        [
            pltpu.VMEM((32 * 64, 128), F32),
            pltpu.VMEM((2 * 16 * 64, 128), F32),
            pltpu.VMEM((XD, 256), F32),
            pltpu.SemaphoreType.DMA(()),
        ],
    )(
        plan,
        far(cells),
        close(rim), close(corner), close(bulk1), close(bulk2), close(ends), close(beside), close(wrap), close(kinds),
    )

    summed = lax.all_to_all(parts, "band", 0, 0)
    potential = call(own_kernel, "own", (shape(CX * CY, CZ),), vmem(1))(field)[0]
    base, tensors, halves = call(
        base_kernel,
        "base",
        (shape(64, 256), shape(2, 128, 256, dtype=BF16), shape(2, 64 * NI, 128, dtype=BF16)),
        anywhere(1) + vmem(5),
    )(parts, rho_ij, coulomb, coupling, close(kinds), projections.reshape(slots * NI, CZ))
    atom_hamiltonian, applied = pl.pallas_call(
        apply_kernel,
        out_shape=(pltpu.HBM((64, 256), F32), pltpu.HBM((64 * NI, 128), F32)),
        in_specs=vmem(5),
        out_specs=tuple(hbm(2)),
        scratch_shapes=[
            pltpu.VMEM((64 * NI, 128), F32),
            pltpu.VMEM((64, 256), F32),
            pltpu.VMEM((64 * NI, 128), F32),
            pltpu.SemaphoreType.DMA((5,)),
        ],
        compiler_params=PARAMS,
        name="apply",
    )(close(summed), close(tensors), close(base), close(kinds), close(halves))
    return (
        potential.reshape(CX, CY, CZ),
        atom_hamiltonian,
        applied.reshape(slots, NI, CZ),
    )


def solution(mesh):
    in_specs = (
        P("dx", "dyz", "band"),
        P("dx", "dyz", "band"),
        P(None, ("dx", "dyz")),
        P(("dx", "dyz")),
        P(("dx", "dyz")),
        P(),
        P(),
        P(),
        P(("dx", "dyz"), None),
        P(("dx", "dyz"), None, "band"),
    )
    out_specs = (P("dx", "dyz", "band"), P(("dx", "dyz"), None), P(("dx", "dyz"), None, "band"))
    return jax.shard_map(local, mesh=mesh, in_specs=in_specs, out_specs=out_specs, check_vma=False)
```
